256 devices in a mesh: blocks: 64 (over z, y, core), obj: 4 (over x).
Axes of the slice: x: 4, y: 4, z: 8, core: 2. Of those that a mesh axis runs over, the one named last changes fastest.
Arguments:
- start_adjoint: float32 [4, 5, 4096, 128], P('obj', None, 'blocks'), may hold values from -6 to 6
- adjoint_source: float32 [4, 5, 4096, 128], P('obj', None, 'blocks'), may hold values from -6 to 6
- block_inverse: float32 [5, 5, 4096, 128], P(None, None, 'blocks'), may hold values from -0.12 to 0.8
- coupling: float32 [4, 4096, 128], P(None, 'blocks'), may hold values from 0.02 to 0.15
- send_cell: int32 [262144], P('blocks'), may hold values from 0 to 8191
- face_peer: int32 [262144, 1], P('blocks'), may hold values from 0 to 63; in each aligned block of 4096 rows (0 to 4095, 4096 to 8191, ...) at most 128 rows name the same one
- receive_cell: int32 [262144], P('blocks'), may hold values from 0 to 8191
- face_weight: float32 [262144], P('blocks'), may hold values from 0.05 to 0.3
- surface_cell: int32 [524288], P('blocks'), may hold values from 0 to 8191
- surface_grad: float32 [3, 5, 524288], P(None, None, 'blocks'), may hold values from -6 to 6
- objective_weight: float32 [4], replicated, may hold values from 0.25 to 1
- deform_owner: int32 [524288, 1], P(('blocks', 'obj')), may hold values from 0 to 63; in each aligned block of 2048 rows (0 to 2047, 2048 to 4095, ...) at most 64 rows name the same one
- deform_node: int32 [524288], P(('blocks', 'obj')), may hold values from 0 to 16383
- mesh_start: float32 [3, 256, 128, 128], P(None, 'blocks', 'obj'), may hold values from -6 to 6
- stiffness: float32 [256, 128, 128], P('blocks', 'obj'), may hold values from 0.1 to 2
Outputs:
- flow_adjoint: float32 [4, 5, 4096, 128], P('obj', None, 'blocks')
- mesh_adjoint: float32 [3, 256, 128, 128], P(None, 'blocks', 'obj')
The draws below stay inside these ranges and needn't reach their ends.
Inputs may be any that keep to these rules, and one draw needn't show every extreme that they name: `face_peer`: among the 4096 rows of one index of blocks no block is named more than 128 times, and this bound is reached. `deform_owner`: among the 2048 rows of one device no block is named more than 64 times, and this bound is reached.
All inputs are finite; a program needn't handle non-finite values.
Results may differ from the reference program's by a relative error of at most 0.0001.
Values sent between devices are 32-bit elements; how exact they have to be, the bound alone decides.
A program may use at most 192 MiB of HBM per device.

```python
import math
import jax
import jax.numpy as jnp
import numpy as np

FIELDS = 5
COMPS = 3
OBJS = 4
FLOW_SWEEPS = 3
DEF_SWEEPS = 2
CY = 64
CZ = 128
FACES = 4096
SURF = 8192
DX = 4
DY = 32
DZ = 128
FCAP = 128
SURFQ = 2048
RCAP = 64
CELLS = 8192
FLOW_ROWS = 4096
FACE_ROWS = 262144
SURF_ROWS = 524288
DEF_X = 256
DEF_Y = 128
N_BLOCKS = 64
N_OBJ = 4


def draw_block_inverse(key, part):
    key_off, key_diag = jax.random.split(key)
    shape_full = (FIELDS, FIELDS, FLOW_ROWS, CZ)
    off_diag = jax.random.uniform(key_off, shape_full, jnp.float32, -0.12, 0.12)
    diagonal = jax.random.uniform(key_diag, shape_full, jnp.float32, 0.5, 0.8)
    identity = (jnp.arange(FIELDS)[:, None] == jnp.arange(FIELDS)[None, :]).astype(jnp.float32)[:, :, None, None]
    return identity * diagonal + (1.0 - identity) * off_diag


def set_ends(entries, key, low, top_value):
    index_at = [jax.random.randint(jax.random.fold_in(key, axis), (), 0, length) for axis, length in enumerate(entries.shape)]
    longest = entries.shape.index(max(entries.shape))
    beside = index_at[:longest] + [(index_at[longest] + 1) % entries.shape[longest]] + index_at[longest + 1:]
    return entries.at[tuple(index_at)].set(low).at[tuple(beside)].set(top_value)


def steps_of(own_key, dims, cuts, least, high):
    gain = 1.0
    for dim, parts in cuts:
        heights = jax.random.uniform(jax.random.fold_in(jax.random.fold_in(own_key, 6), dim), (parts,), jnp.float32, least / len(cuts), high / len(cuts))
        gain = gain * jnp.repeat(jnp.exp(heights), dims[dim] // parts).reshape((-1,) + (1,) * (len(dims) - 1 - dim))
    return gain


def shared_out(rng, own, number, rows, number_of, top, most, slope):
    ranking = jax.random.permutation(rng, number_of)
    crowded, common = portions_of(number_of, rows * top, most, slope, True), portions_of(number_of, rows * top, most, slope, False)
    places = jnp.arange(number_of)

    def named(tallies, turn):
        used = int((tallies > 0).sum())
        fixed = max(1, used // 4)
        moved = fixed + (places - fixed + turn * (used - fixed)) % max(1, number_of - fixed)
        return jnp.zeros((number_of,), jnp.int32).at[ranking[jnp.where(places < fixed, places, moved)]].set(jnp.asarray(tallies, jnp.int32))

    tallies = jnp.where(number % 4 == 0, named(crowded, number // 4), named(common, number - number // 4 - 1))
    mixed = jax.random.permutation(jax.random.fold_in(own, 3), number_of)
    donor, taker = mixed[0:number_of // 2 * 2:2], mixed[1:number_of // 2 * 2:2]
    room = jnp.minimum(tallies[donor] - 1, most - tallies[taker]) // 2
    room = jnp.where((donor == ranking[0]) | (taker == ranking[0]) | (tallies[taker] == 0), 0, jnp.maximum(room, 0))
    moved = jax.random.randint(jax.random.fold_in(own, 4), (number_of // 2,), 0, 1 << 20) % (room + 1)
    tallies = tallies.at[donor].add(-moved).at[taker].add(moved)
    members = jnp.searchsorted(jnp.cumsum(tallies), jnp.arange(rows * top), side="right").astype(jnp.int32)
    table = members.reshape(top, rows).T
    table = table[jax.random.permutation(jax.random.fold_in(own, 1), rows)]
    turn = jax.random.randint(jax.random.fold_in(own, 2), (rows, 1), 0, top)
    return jnp.take_along_axis(table, (jnp.arange(top)[None, :] + turn) % top, axis=1)


def portions_of(number_of, total, most, skew, full):
    portions = [(1 << 20) // math.isqrt(rank ** skew) + 1 for rank in range(1, number_of + 1)]
    largest = most if full else min(most, max(-(-total // number_of), total * portions[0] // sum(portions)))
    least = 1 if total - largest >= number_of - 1 else 0
    holding, surplus = [largest] + [least] * (number_of - 1), total - largest - least * (number_of - 1)
    while surplus > 0:
        free = [i for i in range(1, number_of) if holding[i] < largest] or [i for i in range(1, number_of) if holding[i] < most]
        pool, left = sum([portions[i] for i in free]), surplus
        for i in free:
            addition = min(most - holding[i], max(1, left * portions[i] // pool), surplus)
            holding[i] = holding[i] + addition
            surplus = surplus - addition
    return np.array(holding)


def centred(stream_key, dims, spread, bound, cuts=(), held_as=jnp.bfloat16):
    array = jax.random.normal(stream_key, dims, jnp.float32) * spread
    if len(cuts) > 0:
        array = steps_of(stream_key, dims, cuts, -0.22, 0.18) * array
    return jnp.clip(array, min=-bound, max=bound).astype(held_as)


def setup_inputs(seed: int = 0) -> dict:
    arg_keys = jax.random.split(jax.random.key(seed), 16)
    start_adjoint = centred(arg_keys[0], (OBJS, FIELDS, FLOW_ROWS, CZ), 1.0, 6.0, ((0, 4), (2, 64)), jnp.float32)
    adjoint_source = centred(arg_keys[1], (OBJS, FIELDS, FLOW_ROWS, CZ), 1.0, 6.0, ((0, 4), (2, 64)), jnp.float32)
    block_inverse = draw_block_inverse(jax.random.fold_in(arg_keys[15], 71), 0)
    coupling = jnp.clip(jnp.exp(math.log(0.15) - 2.014903 * jax.random.uniform(arg_keys[3], (4, FLOW_ROWS, CZ), jnp.float32) ** steps_of(arg_keys[3], (4, FLOW_ROWS, CZ), ((1, 64),), -0.2, 0.2)), 0.02, 0.15)
    send_cell = set_ends(jax.random.randint(arg_keys[4], (FACE_ROWS,), 0, CELLS), jax.random.fold_in(arg_keys[4], 1), 0, CELLS - 1).astype(jnp.int32)
    face_peer_keys = jax.random.split(jax.random.fold_in(arg_keys[5], 1), FACE_ROWS // FACES)
    face_peer_turns = jax.random.permutation(jax.random.fold_in(arg_keys[5], 3), FACE_ROWS // FACES)
    face_peer = jax.vmap(lambda own, number: shared_out(jax.random.fold_in(arg_keys[5], 2), own, number, FACES, N_BLOCKS, 1, FCAP, 1))(face_peer_keys, face_peer_turns).reshape((FACE_ROWS, 1))
    receive_cell = set_ends(jax.random.randint(arg_keys[6], (FACE_ROWS,), 0, CELLS), jax.random.fold_in(arg_keys[6], 1), 0, CELLS - 1).astype(jnp.int32)
    face_weight = jnp.clip(jnp.exp(math.log(0.3) - 1.7917595 * jax.random.uniform(arg_keys[7], (FACE_ROWS,), jnp.float32) ** steps_of(arg_keys[7], (FACE_ROWS,), ((0, 64),), -0.2, 0.2)), 0.05, 0.3)
    surface_cell = set_ends(jax.random.randint(arg_keys[8], (SURF_ROWS,), 0, CELLS), jax.random.fold_in(arg_keys[8], 1), 0, CELLS - 1).astype(jnp.int32)
    surface_grad = centred(arg_keys[9], (COMPS, FIELDS, SURF_ROWS), 1.0, 6.0, ((2, 64),), jnp.float32)
    objective_weight = jnp.clip(jnp.exp(jax.random.uniform(arg_keys[10], (OBJS,), jnp.float32, math.log(0.25), math.log(1.0))), 0.25, 1.0)
    deform_owner_keys = jax.random.split(jax.random.fold_in(arg_keys[11], 1), SURF_ROWS // SURFQ)
    deform_owner_turns = jax.random.permutation(jax.random.fold_in(arg_keys[11], 3), SURF_ROWS // SURFQ)
    deform_owner = jax.vmap(lambda own, number: shared_out(jax.random.fold_in(arg_keys[11], 2), own, number, SURFQ, N_BLOCKS, 1, RCAP, 1))(deform_owner_keys, deform_owner_turns).reshape((SURF_ROWS, 1))
    deform_node = set_ends(jax.random.randint(arg_keys[12], (SURF_ROWS,), 0, DX * DY * DZ), jax.random.fold_in(arg_keys[12], 1), 0, (DX * DY * DZ) - 1).astype(jnp.int32)
    mesh_start = centred(arg_keys[13], (COMPS, DEF_X, DEF_Y, DZ), 1.0, 6.0, ((1, 64), (2, 4)), jnp.float32)
    stiffness = jnp.clip(jnp.exp(math.log(2.0) - 2.9957323 * jax.random.uniform(arg_keys[14], (DEF_X, DEF_Y, DZ), jnp.float32) ** steps_of(arg_keys[14], (DEF_X, DEF_Y, DZ), ((0, 64), (1, 4)), -0.2, 0.2)), 0.1, 2.0)
    return {"start_adjoint": start_adjoint, "adjoint_source": adjoint_source, "block_inverse": block_inverse, "coupling": coupling, "send_cell": send_cell, "face_peer": face_peer, "receive_cell": receive_cell, "face_weight": face_weight, "surface_cell": surface_cell, "surface_grad": surface_grad, "objective_weight": objective_weight, "deform_owner": deform_owner, "deform_node": deform_node, "mesh_start": mesh_start, "stiffness": stiffness}


OMEGA = 0.8


def flow_interior(adjoint, couple_coef):
    zero_rows = jnp.zeros_like(adjoint[:, :, :, :1, :])
    below = jnp.concatenate([zero_rows, adjoint[:, :, :, :-1, :]], axis=3)
    above = jnp.concatenate([adjoint[:, :, :, 1:, :], zero_rows], axis=3)
    zero_cols = jnp.zeros_like(adjoint[..., :1])
    left_side = jnp.concatenate([zero_cols, adjoint[..., :-1]], axis=4)
    right_side = jnp.concatenate([adjoint[..., 1:], zero_cols], axis=4)
    return couple_coef[0] * below + couple_coef[1] * above + couple_coef[2] * left_side + couple_coef[3] * right_side


def apply_inverse(matrix, vector):
    stacked_rows = []
    for row_idx in range(matrix.shape[0]):
        accum_sum = matrix[row_idx, 0] * vector[:, 0]
        for col_idx in range(1, matrix.shape[1]):
            accum_sum = accum_sum + matrix[row_idx, col_idx] * vector[:, col_idx]
        stacked_rows.append(accum_sum)
    return jnp.stack(stacked_rows, axis=1)


def reference(start_adjoint, adjoint_source, block_inverse, coupling, send_cell, face_peer, receive_cell, face_weight, surface_cell, surface_grad, objective_weight, deform_owner, deform_node, mesh_start, stiffness):
    block_count = N_BLOCKS
    cell_count = CY * CZ
    flow_shape = (OBJS, FIELDS, block_count, CY, CZ)
    adjoint = start_adjoint.reshape(flow_shape)
    source_term = adjoint_source.reshape(flow_shape)
    block_inv = block_inverse.reshape(FIELDS, FIELDS, block_count, CY, CZ)
    couple_coef = coupling.reshape(4, block_count, CY, CZ)
    owner_rows = jnp.arange(block_count * FACES, dtype=jnp.int32) // FACES
    source = owner_rows * cell_count + send_cell
    target = face_peer[:, 0] * cell_count + receive_cell
    for sweep_idx in range(FLOW_SWEEPS):
        flat_cells = adjoint.reshape(OBJS, FIELDS, block_count * cell_count)
        sent_values = flat_cells[:, :, source] * face_weight
        face_terms = jnp.zeros_like(flat_cells).at[:, :, target].add(sent_values).reshape(flow_shape)
        total_term = source_term + flow_interior(adjoint, couple_coef) + face_terms
        adjoint = (1.0 - OMEGA) * adjoint + OMEGA * apply_inverse(block_inv, total_term)
    flow_adjoint = adjoint.reshape(OBJS, FIELDS, block_count * CY, CZ)
    flat_cells = adjoint.reshape(OBJS, FIELDS, block_count * cell_count)
    row_ids = jnp.arange(block_count * SURF, dtype=jnp.int32)
    surface_values = flat_cells[:, :, (row_ids // SURF) * cell_count + surface_cell]
    combined = jnp.zeros((COMPS, block_count * SURF), jnp.float32)
    for obj_idx in range(OBJS):
        sensitivity = jnp.sum(surface_grad * surface_values[obj_idx][None], axis=1)
        combined = combined + objective_weight[obj_idx] * sensitivity
    quarter = (row_ids % SURF) // SURFQ
    owner_block = deform_owner[:, 0]
    node_x = owner_block * DX + deform_node // (DY * DZ)
    node_y = quarter * DY + (deform_node // DZ) % DY
    node_z = deform_node % DZ
    surface_force = jnp.zeros((COMPS, block_count * DX, N_OBJ * DY, DZ), jnp.float32).at[:, node_x, node_y, node_z].add(combined)
    mesh_field = mesh_start
    for sweep_idx in range(DEF_SWEEPS):
        padded = jnp.pad(mesh_field, ((0, 0), (1, 1), (1, 1), (1, 1)))
        beside = padded[:, 2:, 1:-1, 1:-1] + padded[:, :-2, 1:-1, 1:-1]
        beside = beside + padded[:, 1:-1, 2:, 1:-1] + padded[:, 1:-1, :-2, 1:-1]
        beside = beside + padded[:, 1:-1, 1:-1, 2:] + padded[:, 1:-1, 1:-1, :-2]
        mesh_field = (1.0 - OMEGA) * mesh_field + OMEGA * (surface_force + beside) / (6.0 + stiffness)
    return flow_adjoint, mesh_field
```

```python
import functools

import jax
import jax.numpy as jnp
from jax import lax
from jax.experimental import pallas as pl
from jax.experimental.pallas import tpu as pltpu
from jax.sharding import PartitionSpec as P

OMEGA = 0.8
SWEEPS = 3
GROUPS = 4

f32, bf16, i32 = jnp.float32, jnp.bfloat16, jnp.int32
LANES = 128
WIDE = 256


def dot(a, b):
    return lax.dot_general(a, b, (((1,), (0,)), ((), ())), preferred_element_type=f32)


def dot_nt(a, b):
    return lax.dot_general(a, b, (((1,), (1,)), ((), ())), preferred_element_type=f32)


def iota(shape, dim):
    return lax.broadcasted_iota(i32, shape, dim)


def fiota(shape, dim):
    return iota(shape, dim).astype(f32)


def halves(x):
    high = x.astype(bf16).astype(f32)
    return high, x - high


def pair(array, k):
    return jnp.concatenate([array[2 * k : 2 * k + 1], array[2 * k + 1 : 2 * k + 2]], axis=1)


def pair_at(ref, k):
    return jnp.concatenate([ref[pl.ds(2 * k, 1), :], ref[pl.ds(2 * k + 1, 1), :]], axis=1)


def bucket_ranks(bucket, chunks, buckets, lhs):
    before = jnp.zeros((buckets, WIDE), f32)
    ids = iota((buckets, WIDE), 0)
    hots = []
    for g in range(chunks):
        hot = jnp.where(ids == pair(bucket, g), 1.0, 0.0)
        rows = slice(g * buckets, (g + 1) * buckets)
        lhs[rows, 0:WIDE] = hot.astype(bf16)
        lhs[rows, WIDE : 2 * WIDE] = before.astype(bf16)
        before = before + hot
    a, b = iota((2 * WIDE, WIDE), 0), iota((2 * WIDE, WIDE), 1)
    upto = jnp.where((a <= b) | (a >= WIDE), 1.0, 0.0).astype(bf16)
    counts = dot(lhs[0 : chunks * buckets, :], upto)
    ranks = []
    for g in range(chunks):
        hot = jnp.where(ids == pair(bucket, g), 1.0, 0.0)
        ranks.append(jnp.sum(counts[g * buckets : (g + 1) * buckets] * hot, axis=0, keepdims=True) - 1.0)
    return ranks


def slot_maps(row_of, rows, ranks, values, lhs, hot_slot):
    ids = iota((rows, WIDE), 0)
    slots = fiota((LANES, WIDE), 0)
    chunks = len(ranks)
    for g in range(chunks):
        lanes = slice(g * WIDE, (g + 1) * WIDE)
        hot_slot[:, lanes] = jnp.where(slots == ranks[g], 1.0, 0.0).astype(bf16)
        mask = ids == pair(row_of, g)
        for j, value in enumerate(values):
            lhs[j * rows : (j + 1) * rows, lanes] = jnp.where(mask, pair(value, g), 0.0).astype(bf16)
    return dot_nt(lhs[0 : len(values) * rows, 0 : chunks * WIDE], hot_slot[:, 0 : chunks * WIDE])


def shifted(x, shift, axis):
    size = x.shape[axis]
    at = iota(x.shape, axis)
    edge = 0 if shift == 1 else size - 1
    return jnp.where(at == edge, 0.0, pltpu.roll(x, 1 if shift == 1 else size - 1, axis))


def kernel(
    n_blocks, n_obj, fields, rows_y, faces, surf, comps, size_x, size_y,
    start_ref, source_hbm, binv_hbm, coup_hbm, send_ref, peer_ref, recv_ref, wgt_ref, scell_ref, grad_hbm, oweight_ref,
    owner_ref, node_ref, mesh_hbm, stiff_hbm,
    flow_hbm, meshout_hbm,
    source, binv, coup, grad, mesh0, stiff,
    rank_lhs, map_lhs, map_hot, scol_m, srow_m, wgt_m,
    chot, wmask, surf_hot, surf_mask, lam, xhl, local,
    sbuf0, rbuf0, sbuf1, rbuf1, recv_hot, recv_lhs,
    ssend, srecv, comb, vhl,
    rcol_m, rrow_m, relay_hot, relay_mask, isend, irecv, vsend, vrecv, node_hot, node_lhs, inode,
    mesh1, mesh2, base, coef, ysend, yrecv, xrecv,
    in_sem, out_sem, self_sem, send_sem, recv_sem, obj_send, obj_recv, halo_send, halo_recv,
):
    b, o = lax.axis_index("blocks"), lax.axis_index("obj")
    chips = n_blocks // 2
    chip, core = b // 2, b % 2
    half_y = rows_y // 2
    group = chips // GROUPS
    quarter = surf // n_obj
    qrows = quarter // LANES

    barrier = pltpu.get_barrier_semaphore()

    def greet(t, carry):
        pl.semaphore_signal(barrier, inc=1, device_id={"blocks": lax.rem(b + t, n_blocks)})
        return carry

    lax.fori_loop(1, n_blocks, greet, 0)
    for s in range(1, n_obj):
        pl.semaphore_signal(barrier, inc=1, device_id={"obj": lax.rem(o + s, n_obj)})

    loads = []
    for k, (src, dst) in enumerate(
        ((source_hbm, source), (coup_hbm, coup), (binv_hbm, binv), (mesh_hbm, mesh0), (stiff_hbm, stiff), (grad_hbm, grad))
    ):
        copy = pltpu.make_async_copy(src, dst, in_sem.at[k])
        copy.start()
        loads.append(copy)

    peer = peer_ref[...]
    slot_row = (((peer >> 1) - chip) & (chips - 1)) * 2 + (peer & 1)
    ranks = bucket_ranks(slot_row, faces // WIDE, n_blocks, rank_lhs)
    send, recv, wgt = send_ref[...], recv_ref[...], wgt_ref[...]
    w_high, w_low = halves(wgt)
    recv_row = recv >> 7
    maps = slot_maps(
        slot_row,
        n_blocks,
        ranks,
        (
            (send >> 7).astype(f32),
            (send & 127).astype(f32),
            w_high,
            w_low,
            (recv_row & (half_y - 1)).astype(f32),
            (recv & 127).astype(f32),
            jnp.where(recv_row >= half_y, 128.0, 0.0),
        ),
        map_lhs,
        map_hot,
    )
    nb = n_blocks
    srow_m[...] = maps[0:nb]
    scol_m[...] = maps[nb : 2 * nb]
    wgt_m[...] = maps[2 * nb : 3 * nb] + maps[3 * nb : 4 * nb]
    sbuf0[:, fields, :] = maps[4 * nb : 5 * nb]
    sbuf0[:, fields + 1, :] = maps[5 * nb : 6 * nb] + maps[6 * nb : 7 * nb]

    def build(t, carry):
        hot = jnp.where(fiota((LANES, WIDE), 0) == pair_at(scol_m, t), 1.0, 0.0).astype(bf16)
        chot[t, 0:LANES] = hot
        chot[t, LANES:WIDE] = hot
        wmask[t] = jnp.where(fiota((rows_y, WIDE), 0) == pair_at(srow_m, t), pair_at(wgt_m, t), 0.0)
        return carry

    lax.fori_loop(0, chips, build, 0)

    def set_lam(value):
        lam[...] = value
        high, low = halves(value)
        xhl[:, 0:LANES] = high.astype(bf16)
        xhl[:, LANES:WIDE] = low.astype(bf16)

    def gathered(hot, mask):
        found = dot(xhl[...], hot).reshape(fields, rows_y, WIDE)
        return jnp.sum(found * mask[None], axis=1)

    set_lam(start_ref[...].reshape(fields * rows_y, LANES))

    def to_chip(t, k):
        return lax.rem(chip + t, chips) * 2 + k

    def send_sweep(sweep):
        sb, rb = (sbuf0, rbuf0) if sweep == 0 else (sbuf1.at[sweep - 1], rbuf1.at[sweep - 1])

        def fill(t):
            value = gathered(chot[t], wmask[t])
            sb[2 * t, 0:fields] = value[:, 0:LANES]
            sb[2 * t + 1, 0:fields] = value[:, LANES:WIDE]

        def body(t, carry):
            fill(t)
            for k in range(2):
                pltpu.make_async_remote_copy(
                    src_ref=sb.at[2 * t + k],
                    dst_ref=rb.at[2 * t + core],
                    send_sem=send_sem.at[sweep],
                    recv_sem=recv_sem.at[sweep, t // group],
                    device_id={"blocks": to_chip(t, k)},
                ).start()
            return carry

        lax.fori_loop(1, chips, body, 0)
        fill(0)
        pltpu.make_async_remote_copy(
            src_ref=sb.at[1 - core],
            dst_ref=rb.at[core],
            send_sem=send_sem.at[sweep],
            recv_sem=recv_sem.at[sweep, 0],
            device_id={"blocks": to_chip(0, 1 - core)},
        ).start()
        pltpu.make_async_copy(sb.at[core], rb.at[core], recv_sem.at[sweep, 0]).start()

    def wait_for(ref, sem):
        pltpu.make_async_copy(ref, ref, sem).wait()

    def receive(sweep):
        rb = rbuf0 if sweep == 0 else rbuf1.at[sweep - 1]
        total = jnp.zeros((2 * fields * half_y, WIDE), f32)
        for g in range(GROUPS):
            wait_for(rb.at[pl.ds(2 * group * g, 2 * group)], recv_sem.at[sweep, g])

            def place(t, carry):
                lanes = pl.ds(pl.multiple_of(t * WIDE, WIDE), WIDE)
                first, second = rb[2 * t], rb[2 * t + 1]
                where = jnp.concatenate([rbuf0[2 * t, fields:], rbuf0[2 * t + 1, fields:]], axis=1)
                if sweep == 0:
                    recv_hot[:, lanes] = jnp.where(fiota((WIDE, WIDE), 0) == where[1:2], 1.0, 0.0).astype(bf16)
                mask = fiota((half_y, WIDE), 0) == where[0:1]
                value = jnp.concatenate([first[0:fields], second[0:fields]], axis=1)
                for part, these in enumerate(halves(value)):
                    for f in range(fields):
                        at = (part * fields + f) * half_y
                        recv_lhs[at : at + half_y, lanes] = jnp.where(mask, these[f : f + 1], 0.0).astype(bf16)
                return carry

            lax.fori_loop(group * g, group * (g + 1), place, 0)
            lanes = slice(group * g * WIDE, group * (g + 1) * WIDE)
            total = total + dot_nt(recv_lhs[:, lanes], recv_hot[:, lanes])
        both = total[0 : fields * half_y] + total[fields * half_y :]
        face = []
        for f in range(fields):
            part = both[f * half_y : (f + 1) * half_y]
            face.append(jnp.concatenate([part[:, 0:LANES], part[:, LANES:WIDE]], axis=0))
        return face

    def update(face):
        rhs = [local[f] + face[f] for f in range(fields)]
        new = []
        for f in range(fields):
            acc = binv[f, 0] * rhs[0]
            for g in range(1, fields):
                acc = acc + binv[f, g] * rhs[g]
            new.append((1.0 - OMEGA) * lam[f * rows_y : (f + 1) * rows_y] + OMEGA * acc)
        set_lam(jnp.concatenate(new, axis=0))

    def local_terms():
        for f in range(fields):
            x = lam[f * rows_y : (f + 1) * rows_y]
            interior = coup[0] * shifted(x, 1, 0) + coup[1] * shifted(x, -1, 0)
            interior = interior + coup[2] * shifted(x, 1, 1) + coup[3] * shifted(x, -1, 1)
            local[f] = source[f] + interior

    pl.semaphore_wait(barrier, n_blocks - 1 + n_obj - 1)

    ends = (lax.rem(b + 1, n_blocks), lax.rem(b + n_blocks - 1, n_blocks))
    sides = (lax.rem(o + 1, n_obj), lax.rem(o + n_obj - 1, n_obj))

    def halo_copies(sweep, field):
        copies = []
        for k in range(2):
            edge = size_x - 1 if k == 0 else 0
            copies.append(
                pltpu.make_async_remote_copy(
                    src_ref=field.at[:, edge],
                    dst_ref=xrecv.at[sweep, k],
                    send_sem=halo_send.at[sweep, k],
                    recv_sem=halo_recv.at[sweep, k],
                    device_id={"blocks": ends[k]},
                )
            )
            copies.append(
                pltpu.make_async_remote_copy(
                    src_ref=ysend.at[sweep, k],
                    dst_ref=yrecv.at[sweep, k],
                    send_sem=halo_send.at[sweep, 2 + k],
                    recv_sem=halo_recv.at[sweep, 2 + k],
                    device_id={"obj": sides[k]},
                )
            )
        return copies

    def neighbours(sweep, field):
        x = field[...]
        zero = jnp.zeros((comps, 1, size_y, LANES), f32)
        low = jnp.where(b > 0, xrecv[sweep, 0][:, None], zero)
        high = jnp.where(b < n_blocks - 1, xrecv[sweep, 1][:, None], zero)
        beside = jnp.concatenate([x[:, 1:], high], axis=1) + jnp.concatenate([low, x[:, :-1]], axis=1)
        flat = x.reshape(comps * size_x * size_y, LANES)
        total = flat.shape[0]
        at = iota((comps, size_x, size_y, LANES), 2)
        before = jnp.where(o > 0, yrecv[sweep, 0], 0.0)[:, :, None]
        after = jnp.where(o < n_obj - 1, yrecv[sweep, 1], 0.0)[:, :, None]
        up = pltpu.roll(flat, total - 1, 0).reshape(x.shape)
        down = pltpu.roll(flat, 1, 0).reshape(x.shape)
        beside = beside + jnp.where(at == size_y - 1, after, up) + jnp.where(at == 0, before, down)
        sideways = shifted(flat, -1, 1) + shifted(flat, 1, 1)
        return x, beside + sideways.reshape(x.shape)

    send_sweep(0)
    loads[3].wait()
    ysend[0, 0] = mesh0[:, :, size_y - 1, :]
    ysend[0, 1] = mesh0[:, :, 0, :]
    halos0 = halo_copies(0, mesh0)
    for copy in halos0:
        copy.start()
    loads[0].wait()
    loads[1].wait()
    local_terms()
    loads[2].wait()

    def build_surface(t, carry):
        cell = pair_at(scell_ref, t)
        hot = jnp.where(iota((LANES, WIDE), 0) == (cell & 127), 1.0, 0.0).astype(bf16)
        surf_hot[t, 0:LANES] = hot
        surf_hot[t, LANES:WIDE] = hot
        surf_mask[t] = jnp.where(iota((rows_y, WIDE), 0) == (cell >> 7), 1.0, 0.0)
        return carry

    lax.fori_loop(0, surf // WIDE, build_surface, 0)
    update(receive(0))

    send_sweep(1)
    local_terms()
    owner, node = owner_ref[...], node_ref[...]
    bucket = (((owner >> 1) - chip) & (chips - 1)) * 2 + (owner & 1)
    relay_ranks = bucket_ranks(bucket, quarter // WIDE, n_blocks, rank_lhs)
    cap = LANES // 2
    side = ((owner & 1) ^ core) * cap
    relay_ranks = [rank + pair(side, g).astype(f32) for g, rank in enumerate(relay_ranks)]
    node_row = node >> 7
    half_nodes = size_x * size_y // 2
    relay_maps = slot_maps(
        bucket >> 1,
        chips,
        relay_ranks,
        (
            fiota((qrows, LANES), 0) + 1.0,
            fiota((qrows, LANES), 1),
            (node_row & (half_nodes - 1)).astype(f32),
            (node & 127).astype(f32),
            jnp.where(node_row >= half_nodes, 128.0, 0.0),
        ),
        map_lhs,
        map_hot,
    )
    rrow_m[...] = relay_maps[0:chips]
    rcol_m[...] = relay_maps[chips : 2 * chips]
    isend[:, 0, :] = relay_maps[2 * chips : 3 * chips]
    isend[:, 1, :] = relay_maps[3 * chips : 4 * chips] + relay_maps[4 * chips : 5 * chips]

    def relay_send(sb, rb, which, before):
        def post(t):
            for k in range(2):
                pltpu.make_async_remote_copy(
                    src_ref=sb.at[t],
                    dst_ref=rb.at[2 * t + core],
                    send_sem=send_sem.at[which],
                    recv_sem=recv_sem.at[which, 0],
                    device_id={"blocks": to_chip(t, k)},
                ).start()

        def body(u, carry):
            before(u)
            post(2 * u)
            post(2 * u + 1)
            return carry

        lax.fori_loop(1, chips // 2, body, 0)
        before(0)
        post(1)
        pltpu.make_async_remote_copy(
            src_ref=sb.at[0],
            dst_ref=rb.at[core],
            send_sem=send_sem.at[which],
            recv_sem=recv_sem.at[which, 0],
            device_id={"blocks": to_chip(0, 1 - core)},
        ).start()
        pltpu.make_async_copy(sb.at[0], rb.at[core], recv_sem.at[which, 0]).start()

    relay_send(isend, irecv, SWEEPS, lambda u: None)

    def build_relay(u, carry):
        hot = jnp.where(fiota((LANES, WIDE), 0) == pair_at(rcol_m, u), 1.0, 0.0).astype(bf16)
        relay_hot[u, 0:LANES] = hot
        relay_hot[u, LANES:WIDE] = hot
        relay_mask[u] = jnp.where(fiota((qrows, WIDE), 0) + 1.0 == pair_at(rrow_m, u), 1.0, 0.0)
        return carry

    lax.fori_loop(0, chips // 2, build_relay, 0)
    update(receive(1))

    send_sweep(2)
    local_terms()
    loads[4].wait()
    for copy in halos0:
        copy.wait_recv()
    coef[...] = OMEGA / (6.0 + stiff[...])
    centre, beside = neighbours(0, mesh0)
    base[...] = (1.0 - OMEGA) * centre + coef[...][None] * beside

    wait_for(irecv, recv_sem.at[SWEEPS, 0])
    mine = iota((1, LANES), 1) // cap == core

    def build_nodes(u, carry):
        lanes = pl.ds(pl.multiple_of(u * WIDE, WIDE), WIDE)
        where = jnp.concatenate(
            [jnp.where(mine, irecv[4 * u + 2 * k], irecv[4 * u + 2 * k + 1]) for k in range(2)], axis=1
        )
        inode[u] = where
        node_hot[:, lanes] = jnp.where(fiota((WIDE, WIDE), 0) == where[1:2], 1.0, 0.0).astype(bf16)
        return carry

    lax.fori_loop(0, chips // 2, build_nodes, 0)
    update(receive(2))
    flow_copy = pltpu.make_async_copy(lam, flow_hbm, out_sem.at[0])
    flow_copy.start()

    loads[5].wait()
    weight = oweight_ref[o]
    obj_copies = []
    for s in list(range(1, n_obj)) + [0]:
        q = lax.rem(o + s, n_obj)

        def surface(k, carry):
            t = q * (qrows // 2) + k
            value = gathered(surf_hot[t], surf_mask[t])
            lanes = pl.ds(pl.multiple_of(t * WIDE, WIDE), WIDE)
            part = grad[0, :, lanes] * value[0:1]
            for f in range(1, fields):
                part = part + grad[f, :, lanes] * value[f : f + 1]
            part = part * weight
            ssend[s, 2 * k] = part[:, 0:LANES]
            ssend[s, 2 * k + 1] = part[:, LANES:WIDE]
            return carry

        lax.fori_loop(0, qrows // 2, surface, 0)
        if s:
            copy = pltpu.make_async_remote_copy(
                src_ref=ssend.at[s],
                dst_ref=srecv.at[s - 1],
                send_sem=obj_send.at[s - 1],
                recv_sem=obj_recv.at[s - 1],
                device_id={"obj": q},
            )
            copy.start()
            obj_copies.append(copy)
    for copy in obj_copies:
        copy.wait_recv()
    comb[...] = ssend[0] + srecv[0] + srecv[1] + srecv[2]
    combined = jnp.concatenate([comb[:, c, :] for c in range(comps)], axis=0)
    high, low = halves(combined)
    vhl[:, 0:LANES] = high.astype(bf16)
    vhl[:, LANES:WIDE] = low.astype(bf16)

    def pick(u):
        found = dot(vhl[...], relay_hot[u]).reshape(comps, qrows, WIDE)
        value = jnp.sum(found * relay_mask[u][None], axis=1)
        vsend[2 * u] = value[:, 0:LANES]
        vsend[2 * u + 1] = value[:, LANES:WIDE]

    relay_send(vsend, vrecv, SWEEPS + 1, pick)

    wait_for(vrecv, recv_sem.at[SWEEPS + 1, 0])

    def place_nodes(u, carry):
        lanes = pl.ds(pl.multiple_of(u * WIDE, WIDE), WIDE)
        value = jnp.concatenate(
            [jnp.where(mine, vrecv[4 * u + 2 * k], vrecv[4 * u + 2 * k + 1]) for k in range(2)], axis=1
        )
        mask = fiota((half_nodes, WIDE), 0) == inode[u][0:1]
        for part, these in enumerate(halves(value)):
            for c in range(comps):
                at = (part * comps + c) * half_nodes
                node_lhs[at : at + half_nodes, lanes] = jnp.where(mask, these[c : c + 1], 0.0).astype(bf16)
        return carry

    lax.fori_loop(0, chips // 2, place_nodes, 0)
    forces = dot_nt(node_lhs[...], node_hot[...])
    forces = forces[0 : comps * half_nodes] + forces[comps * half_nodes :]
    forces = forces.reshape(comps, size_x // 2, size_y, WIDE)
    force = jnp.concatenate([forces[..., 0:LANES], forces[..., LANES:WIDE]], axis=1)

    scaled = coef[...][None] * force
    first = base[...] + scaled
    mesh1[...] = first
    ysend[1, 0] = mesh1[:, :, size_y - 1, :]
    ysend[1, 1] = mesh1[:, :, 0, :]
    halos1 = halo_copies(1, mesh1)
    for copy in halos1:
        copy.start()
    for copy in halos1:
        copy.wait_recv()
    centre, beside = neighbours(1, mesh1)
    mesh2[...] = (1.0 - OMEGA) * centre + scaled + coef[...][None] * beside
    mesh_copy = pltpu.make_async_copy(mesh2, meshout_hbm, out_sem.at[1])
    mesh_copy.start()

    for copy in halos0 + halos1 + obj_copies:
        copy.wait_send()
    wait_for(sbuf0.at[pl.ds(0, n_blocks - 1)], send_sem.at[0])
    for sweep in range(1, SWEEPS):
        wait_for(sbuf1.at[sweep - 1, pl.ds(0, n_blocks - 1)], send_sem.at[sweep])
    for sb, which in ((irecv, SWEEPS), (vrecv, SWEEPS + 1)):
        wait_for(sb.at[pl.ds(0, n_blocks - 1)], send_sem.at[which])
    flow_copy.wait()
    mesh_copy.wait()


def shards(
    n_blocks, n_obj, start, source, binv, coup, send, peer, recv, wgt, scell, grad, oweight, owner, node, mesh, stiff
):
    _, fields, rows_y, cols = start.shape
    faces, surf = send.shape[0], scell.shape[0]
    comps, size_x, size_y, _ = mesh.shape
    quarter = surf // n_obj
    qrows = quarter // LANES
    chips = n_blocks // 2
    half_nodes = size_x * size_y // 2
    vmem = pl.BlockSpec(memory_space=pltpu.VMEM)
    smem = pl.BlockSpec(memory_space=pltpu.SMEM)
    hbm = pl.BlockSpec(memory_space=pl.ANY)
    V = pltpu.VMEM
    dma = pltpu.SemaphoreType.DMA
    call = pl.pallas_call(
        functools.partial(kernel, n_blocks, n_obj, fields, rows_y, faces, surf, comps, size_x, size_y),
        out_shape=(
            jax.ShapeDtypeStruct((fields * rows_y, cols), f32),
            jax.ShapeDtypeStruct(mesh.shape, f32),
        ),
        in_specs=[vmem, hbm, hbm, hbm, vmem, vmem, vmem, vmem, vmem, hbm, smem, vmem, vmem, hbm, hbm],
        out_specs=(hbm, hbm),
        scratch_shapes=[
            V((fields, rows_y, cols), f32),
            V(binv.shape, f32),
            V(coup.shape, f32),
            V((fields, comps, surf), f32),
            V(mesh.shape, f32),
            V(stiff.shape, f32),
            V((faces // WIDE * n_blocks, 2 * WIDE), bf16),
            V((7 * n_blocks, faces), bf16),
            V((LANES, faces), bf16),
            V((n_blocks, LANES), f32),
            V((n_blocks, LANES), f32),
            V((n_blocks, LANES), f32),
            V((chips, WIDE, WIDE), bf16),
            V((chips, rows_y, WIDE), f32),
            V((surf // WIDE, WIDE, WIDE), bf16),
            V((surf // WIDE, rows_y, WIDE), f32),
            V((fields * rows_y, LANES), f32),
            V((fields * rows_y, WIDE), bf16),
            V((fields, rows_y, LANES), f32),
            V((n_blocks, fields + 2, LANES), f32),
            V((n_blocks, fields + 2, LANES), f32),
            V((SWEEPS - 1, n_blocks, fields, LANES), f32),
            V((SWEEPS - 1, n_blocks, fields, LANES), f32),
            V((WIDE, chips * WIDE), bf16),
            V((fields * rows_y, chips * WIDE), bf16),
            V((n_obj, qrows, comps, LANES), f32),
            V((n_obj - 1, qrows, comps, LANES), f32),
            V((qrows, comps, LANES), f32),
            V((comps * qrows, WIDE), bf16),
            V((chips, LANES), f32),
            V((chips, LANES), f32),
            V((chips // 2, WIDE, WIDE), bf16),
            V((chips // 2, qrows, WIDE), f32),
            V((chips, 2, LANES), f32),
            V((n_blocks, 2, LANES), f32),
            V((chips, comps, LANES), f32),
            V((n_blocks, comps, LANES), f32),
            V((WIDE, chips * LANES), bf16),
            V((2 * comps * half_nodes, chips * LANES), bf16),
            V((chips // 2, 2, WIDE), f32),
            V(mesh.shape, f32),
            V(mesh.shape, f32),
            V(mesh.shape, f32),
            V(stiff.shape, f32),
            V((2, 2, comps, size_x, LANES), f32),
            V((2, 2, comps, size_x, LANES), f32),
            V((2, 2, comps, size_y, LANES), f32),
            dma((6,)),
            dma((2,)),
            dma((1,)),
            dma((SWEEPS + 2,)),
            dma((SWEEPS + 2, GROUPS)),
            dma((n_obj - 1,)),
            dma((n_obj - 1,)),
            dma((2, 4)),
            dma((2, 4)),
        ],
        compiler_params=pltpu.CompilerParams(
            collective_id=0, has_side_effects=True, vmem_limit_bytes=56 * 1024 * 1024
        ),
    )
    flow, mesh_adjoint = call(
        start[0],
        source[0],
        binv,
        coup,
        send.reshape(-1, LANES),
        peer.reshape(-1, LANES),
        recv.reshape(-1, LANES),
        wgt.reshape(-1, LANES),
        scell.reshape(-1, LANES),
        jnp.transpose(grad, (1, 0, 2)),
        oweight,
        owner.reshape(-1, LANES),
        node.reshape(-1, LANES),
        mesh,
        stiff,
    )
    return flow.reshape(start.shape), mesh_adjoint


def solution(mesh):
    placed = (
        P("obj", None, "blocks", None),
        P("obj", None, "blocks", None),
        P(None, None, "blocks", None),
        P(None, "blocks", None),
        P("blocks"),
        P("blocks", None),
        P("blocks"),
        P("blocks"),
        P("blocks"),
        P(None, None, "blocks"),
        P(),
        P(("blocks", "obj"), None),
        P(("blocks", "obj")),
        P(None, "blocks", "obj", None),
        P("blocks", "obj", None),
    )
    return jax.shard_map(
        functools.partial(shards, mesh.shape["blocks"], mesh.shape["obj"]),
        mesh=mesh,
        in_specs=placed,
        out_specs=(P("obj", None, "blocks", None), P(None, "blocks", "obj", None)),
        check_vma=False,
    )
```

```python
import functools

import jax
import jax.numpy as jnp
from jax import lax
from jax.experimental import pallas as pl
from jax.experimental.pallas import tpu as pltpu
from jax.sharding import PartitionSpec as P

OMEGA = 0.8
SWEEPS = 3
GROUPS = 4
BATCH = 8
CHAIN = 4
RING_Y = 4

f32, bf16, i32 = jnp.float32, jnp.bfloat16, jnp.int32
LANES = 128
WIDE = 256


def dot(a, b):
    return lax.dot_general(a, b, (((1,), (0,)), ((), ())), preferred_element_type=f32)


def dot_nt(a, b):
    return lax.dot_general(a, b, (((1,), (1,)), ((), ())), preferred_element_type=f32)


def iota(shape, dim):
    return lax.broadcasted_iota(i32, shape, dim)


def fiota(shape, dim):
    return iota(shape, dim).astype(f32)


def far_first(i, n):
    return (n // 2 + (1 - 2 * (i % 2)) * ((i + 1) // 2)) % n


def place_of(distance, n):
    d = distance - n // 2
    return jnp.where(d < 0, -2 * d - 1, 2 * d)


def halves(x):
    high = x.astype(bf16).astype(f32)
    return high, x - high


def pair(array, k):
    return jnp.concatenate([array[2 * k : 2 * k + 1], array[2 * k + 1 : 2 * k + 2]], axis=1)


def pair_at(ref, k):
    return jnp.concatenate([ref[pl.ds(2 * k, 1), :], ref[pl.ds(2 * k + 1, 1), :]], axis=1)


def bucket_ranks(bucket, chunks, buckets, lhs):
    before = jnp.zeros((buckets, WIDE), f32)
    ids = iota((buckets, WIDE), 0)
    hots = []
    for g in range(chunks):
        hot = jnp.where(ids == pair(bucket, g), 1.0, 0.0)
        rows = slice(g * buckets, (g + 1) * buckets)
        lhs[rows, 0:WIDE] = hot.astype(bf16)
        lhs[rows, WIDE : 2 * WIDE] = before.astype(bf16)
        before = before + hot
    a, b = iota((2 * WIDE, WIDE), 0), iota((2 * WIDE, WIDE), 1)
    upto = jnp.where((a <= b) | (a >= WIDE), 1.0, 0.0).astype(bf16)
    middle = chunks * buckets // 2
    counts = [dot(lhs[0:middle, :], upto), dot(lhs[middle : 2 * middle, :], upto)]
    ranks = []
    for g in range(chunks):
        hot = jnp.where(ids == pair(bucket, g), 1.0, 0.0)
        at = g % (chunks // 2) * buckets
        ranks.append(jnp.sum(counts[2 * g // chunks][at : at + buckets] * hot, axis=0, keepdims=True) - 1.0)
    return ranks


def slot_maps(row_of, rows, ranks, width, values, lhs, hot_slot):
    ids = iota((rows, WIDE), 0)
    slots = fiota((width, WIDE), 0)
    chunks = len(ranks)
    for g in range(chunks):
        lanes = slice(g * WIDE, (g + 1) * WIDE)
        hot_slot[0:width, lanes] = jnp.where(slots == ranks[g], 1.0, 0.0).astype(bf16)
        mask = ids == pair(row_of, g)
        for j, value in enumerate(values):
            lhs[j * rows : (j + 1) * rows, lanes] = jnp.where(mask, pair(value, g), 0.0).astype(bf16)
    middle, high = chunks * WIDE // 2, len(values) * rows
    first = dot_nt(lhs[0:high, 0:middle], hot_slot[0:width, 0:middle])
    return first + dot_nt(lhs[0:high, middle : 2 * middle], hot_slot[0:width, middle : 2 * middle])


def shifted(x, shift, axis):
    size = x.shape[axis]
    at = iota(x.shape, axis)
    edge = 0 if shift == 1 else size - 1
    return jnp.where(at == edge, 0.0, pltpu.roll(x, 1 if shift == 1 else size - 1, axis))


def kernel(
    n_blocks, n_obj, fields, rows_y, faces, surf, comps, size_x, size_y,
    start_hbm, source_hbm, binv_hbm, coup_hbm, send_hbm, peer_hbm, recv_hbm, wgt_hbm, scell_hbm, grad_hbm, oweight_ref,
    owner_hbm, node_hbm, mesh_hbm, stiff_hbm,
    lam, mesh2,
    source, binv, coup, grad, mesh0, stiff, peer_ref, send_ref, recv_ref, wgt_ref, start_ref, scell_ref, owner_ref, node_ref,
    rank_lhs, map_lhs, map_hot, scol_m, srow_m, wgt_m,
    chot, wmask, surf_hot, surf_mask, xhl, local,
    sbuf0, rbuf0, sbuf1, rbuf1, recv_hot, recv_lhs,
    ssend, srecv, comb, vhl,
    recv_row_m, rcol_m, rrow_m, relay_hot, relay_mask, isend, irecv, vsend, vrecv, node_hot, node_lhs, inode,
    mesh1, base, coef, ysend, yrecv, xrecv,
    in_sem, send_sem, recv_sem, obj_send, obj_recv, halo_send, halo_recv,
):
    b, o = lax.axis_index("blocks"), lax.axis_index("obj")
    chips = n_blocks // 2
    chip, core = b // 2, b % 2
    half_y = rows_y // 2
    group = chips // GROUPS
    quarter = surf // n_obj
    qrows = quarter // LANES

    ring_z = chips // RING_Y
    chip_z, chip_y = chip // RING_Y, chip % RING_Y
    last = chips - 1

    z_part = [lax.rem(chip_z + far_first(i, ring_z), ring_z) * (2 * RING_Y) for i in range(ring_z)]
    y_part = [lax.rem(chip_y + far_first(i, RING_Y), RING_Y) * 2 for i in range(RING_Y)]

    def to_chip(t, k):
        return z_part[t // RING_Y] + y_part[t % RING_Y] + k

    def slot_of(block):
        z = place_of(((block // (2 * RING_Y)) - chip_z) & (ring_z - 1), ring_z)
        y = place_of(((block // 2) - chip_y) & (RING_Y - 1), RING_Y)
        return (z * RING_Y + y) * 2 + (block & 1)

    barrier = pltpu.get_barrier_semaphore()

    loads = []
    for k, (src, dst) in enumerate(
        (
            (source_hbm, source), (coup_hbm, coup), (binv_hbm, binv), (mesh_hbm, mesh0), (stiff_hbm, stiff), (grad_hbm, grad),
            (peer_hbm, peer_ref), (send_hbm, send_ref), (recv_hbm, recv_ref), (wgt_hbm, wgt_ref), (start_hbm, start_ref),
            (scell_hbm, scell_ref), (owner_hbm, owner_ref), (node_hbm, node_ref),
        )
    ):
        loads.append(pltpu.make_async_copy(src, dst, in_sem.at[k]))
    for k in (*range(6, len(loads)), *range(6)):
        loads[k].start()

    for t in range(last):
        for k in range(2):
            pl.semaphore_signal(barrier, inc=1, device_id={"blocks": to_chip(t, k)})
    pl.semaphore_signal(barrier, inc=1, device_id={"blocks": to_chip(last, 1 - core)})
    for s in range(1, n_obj):
        pl.semaphore_signal(barrier, inc=1, device_id={"obj": lax.rem(o + s, n_obj)})

    for k in range(6, 10):
        loads[k].wait()

    peer = peer_ref[...]
    slot_row = slot_of(peer)
    ranks = bucket_ranks(slot_row, faces // WIDE, n_blocks, rank_lhs)
    send, recv, wgt = send_ref[...], recv_ref[...], wgt_ref[...]
    w_high, w_low = halves(wgt)
    side = (slot_row & 1) * LANES
    maps = slot_maps(
        slot_row >> 1,
        chips,
        [rank + pair(side, g).astype(f32) for g, rank in enumerate(ranks)],
        WIDE,
        (
            (send >> 7).astype(f32),
            (send & 127).astype(f32),
            w_high,
            w_low,
            (recv >> 7).astype(f32),
            (recv & 127).astype(f32),
        ),
        map_lhs,
        map_hot,
    )
    srow_m[...] = maps[0:chips]
    scol_m[...] = maps[chips : 2 * chips]
    wgt_m[...] = maps[2 * chips : 3 * chips] + maps[3 * chips : 4 * chips]
    target = maps[4 * chips : 5 * chips] * 128.0 + maps[5 * chips : 6 * chips]
    for t in range(chips):
        sbuf0[2 * t, fields:] = target[t : t + 1, 0:LANES]
        sbuf0[2 * t + 1, fields:] = target[t : t + 1, LANES:WIDE]

    def build(t, carry):
        hot = jnp.where(fiota((LANES, WIDE), 0) == scol_m[pl.ds(t, 1), :], 1.0, 0.0).astype(bf16)
        chot[t, 0:LANES] = hot
        chot[t, LANES:WIDE] = hot
        wmask[t] = jnp.where(fiota((rows_y, WIDE), 0) == srow_m[pl.ds(t, 1), :], wgt_m[pl.ds(t, 1), :], 0.0)
        return carry

    def set_lam(value):
        lam[...] = value
        high, low = halves(value)
        xhl[:, 0:LANES] = high.astype(bf16)
        xhl[:, LANES:WIDE] = low.astype(bf16)

    def gathered(hot, mask):
        found = dot(xhl[...], hot).reshape(fields, rows_y, WIDE)
        return jnp.sum(found * mask[None], axis=1)

    loads[10].wait()
    set_lam(start_ref[...].reshape(fields * rows_y, LANES))

    def send_sweep(sweep):
        sb, rb = (sbuf0, rbuf0) if sweep == 0 else (sbuf1.at[sweep - 1], rbuf1.at[sweep - 1])

        def fill(first):
            values = [gathered(chot[first + j], wmask[first + j]) for j in range(group)]
            for j, value in enumerate(values):
                sb[2 * (first + j), 0:fields] = value[:, 0:LANES]
                sb[2 * (first + j) + 1, 0:fields] = value[:, LANES:WIDE]

        def post(t, g):
            for k in range(2):
                pltpu.make_async_remote_copy(
                    src_ref=sb.at[2 * t + k],
                    dst_ref=rb.at[2 * t + core],
                    send_sem=send_sem.at[sweep],
                    recv_sem=recv_sem.at[sweep, g],
                    device_id={"blocks": to_chip(t, k)},
                ).start()

        for g in range(GROUPS):
            if sweep == 0:
                lax.fori_loop(group * g, group * (g + 1), build, 0)
            fill(group * g)
            if sweep == 0 and g == 0:
                pl.semaphore_wait(barrier, n_blocks - 1 + n_obj - 1)
            for t in range(group * g, min(group * (g + 1), last)):
                post(t, g)
        pltpu.make_async_remote_copy(
            src_ref=sb.at[2 * last + 1 - core],
            dst_ref=rb.at[2 * last + core],
            send_sem=send_sem.at[sweep],
            recv_sem=recv_sem.at[sweep, GROUPS - 1],
            device_id={"blocks": to_chip(last, 1 - core)},
        ).start()
        pltpu.make_async_copy(sb.at[2 * last + core], rb.at[2 * last + core], recv_sem.at[sweep, GROUPS - 1]).start()

    def wait_for(ref, sem):
        pltpu.make_async_copy(ref, ref, sem).wait()

    def receive(sweep):
        rb = rbuf0 if sweep == 0 else rbuf1.at[sweep - 1]
        def place(t):
            lanes = slice(t * WIDE, (t + 1) * WIDE)
            first, second = rb[2 * t], rb[2 * t + 1]
            if sweep == 0:
                cell = jnp.concatenate([first[fields:], second[fields:]], axis=1).astype(i32)
                row = cell >> 7
                col = (cell & 127) + jnp.where(row >= half_y, LANES, 0)
                recv_row_m[t] = row & (half_y - 1)
                recv_hot[:, lanes] = jnp.where(iota((WIDE, WIDE), 0) == col, 1.0, 0.0).astype(bf16)
            mask = iota((half_y, WIDE), 0) == recv_row_m[t]
            value = jnp.concatenate([first[0:fields], second[0:fields]], axis=1)
            for part, these in enumerate(halves(value)):
                for f in range(fields):
                    at = (part * fields + f) * half_y
                    recv_lhs[at : at + half_y, lanes] = jnp.where(mask, these[f : f + 1], 0.0).astype(bf16)

        total = None
        for g in range(GROUPS):
            wait_for(rb.at[pl.ds(2 * group * g, 2 * group)], recv_sem.at[sweep, g])
            if g % 2 == 0:
                continue
            for t in range((g - 1) * group, (g + 1) * group, CHAIN):
                for j in range(CHAIN):
                    place(t + j)
                lanes = slice(t * WIDE, (t + CHAIN) * WIDE)
                part = dot_nt(recv_lhs[:, lanes], recv_hot[:, lanes])
                total = part if total is None else total + part
        both = total[0 : fields * half_y] + total[fields * half_y :]
        face = []
        for f in range(fields):
            part = both[f * half_y : (f + 1) * half_y]
            face.append(jnp.concatenate([part[:, 0:LANES], part[:, LANES:WIDE]], axis=0))
        return face

    def update(face):
        rhs = [local[f] + face[f] for f in range(fields)]
        new = []
        for f in range(fields):
            acc = binv[f, 0] * rhs[0]
            for g in range(1, fields):
                acc = acc + binv[f, g] * rhs[g]
            new.append((1.0 - OMEGA) * lam[f * rows_y : (f + 1) * rows_y] + OMEGA * acc)
        set_lam(jnp.concatenate(new, axis=0))

    def local_terms():
        for f in range(fields):
            x = lam[f * rows_y : (f + 1) * rows_y]
            interior = coup[0] * shifted(x, 1, 0) + coup[1] * shifted(x, -1, 0)
            interior = interior + coup[2] * shifted(x, 1, 1) + coup[3] * shifted(x, -1, 1)
            local[f] = source[f] + interior

    ends = (lax.rem(b + 1, n_blocks), lax.rem(b + n_blocks - 1, n_blocks))
    sides = (lax.rem(o + 1, n_obj), lax.rem(o + n_obj - 1, n_obj))

    def halo_copies(sweep, field):
        copies = []
        for k in range(2):
            edge = size_x - 1 if k == 0 else 0
            copies.append(
                pltpu.make_async_remote_copy(
                    src_ref=field.at[:, edge],
                    dst_ref=xrecv.at[sweep, k],
                    send_sem=halo_send.at[sweep, k],
                    recv_sem=halo_recv.at[sweep, k],
                    device_id={"blocks": ends[k]},
                )
            )
            copies.append(
                pltpu.make_async_remote_copy(
                    src_ref=ysend.at[sweep, k],
                    dst_ref=yrecv.at[sweep, k],
                    send_sem=halo_send.at[sweep, 2 + k],
                    recv_sem=halo_recv.at[sweep, 2 + k],
                    device_id={"obj": sides[k]},
                )
            )
        return copies

    def neighbours(sweep, field):
        x = field[...]
        zero = jnp.zeros((comps, 1, size_y, LANES), f32)
        low = jnp.where(b > 0, xrecv[sweep, 0][:, None], zero)
        high = jnp.where(b < n_blocks - 1, xrecv[sweep, 1][:, None], zero)
        beside = jnp.concatenate([x[:, 1:], high], axis=1) + jnp.concatenate([low, x[:, :-1]], axis=1)
        flat = x.reshape(comps * size_x * size_y, LANES)
        total = flat.shape[0]
        at = iota((comps, size_x, size_y, LANES), 2)
        before = jnp.where(o > 0, yrecv[sweep, 0], 0.0)[:, :, None]
        after = jnp.where(o < n_obj - 1, yrecv[sweep, 1], 0.0)[:, :, None]
        up = pltpu.roll(flat, total - 1, 0).reshape(x.shape)
        down = pltpu.roll(flat, 1, 0).reshape(x.shape)
        beside = beside + jnp.where(at == size_y - 1, after, up) + jnp.where(at == 0, before, down)
        sideways = shifted(flat, -1, 1) + shifted(flat, 1, 1)
        return x, beside + sideways.reshape(x.shape)

    send_sweep(0)
    loads[3].wait()
    ysend[0, 0] = mesh0[:, :, size_y - 1, :]
    ysend[0, 1] = mesh0[:, :, 0, :]
    halos0 = halo_copies(0, mesh0)
    for copy in halos0:
        copy.start()
    loads[0].wait()
    loads[1].wait()
    local_terms()
    loads[2].wait()

    def build_surface(t, carry):
        cell = pair_at(scell_ref, t)
        hot = jnp.where(iota((LANES, WIDE), 0) == (cell & 127), 1.0, 0.0).astype(bf16)
        surf_hot[t, 0:LANES] = hot
        surf_hot[t, LANES:WIDE] = hot
        surf_mask[t] = jnp.where(iota((rows_y, WIDE), 0) == (cell >> 7), 1.0, 0.0)
        return carry

    loads[11].wait()
    lax.fori_loop(0, surf // WIDE, build_surface, 0)
    update(receive(0))

    send_sweep(1)
    local_terms()
    loads[12].wait()
    loads[13].wait()
    owner, node = owner_ref[...], node_ref[...]
    bucket = slot_of(owner)
    relay_ranks = bucket_ranks(bucket, quarter // WIDE, n_blocks, rank_lhs)
    cap = LANES // 2
    side = ((owner & 1) ^ core) * cap
    relay_ranks = [rank + pair(side, g).astype(f32) for g, rank in enumerate(relay_ranks)]
    node_row = node >> 7
    half_nodes = size_x * size_y // 2
    relay_maps = slot_maps(
        bucket >> 1,
        chips,
        relay_ranks,
        LANES,
        (
            fiota((qrows, LANES), 0) + 1.0,
            fiota((qrows, LANES), 1),
            (node_row & (half_nodes - 1)).astype(f32),
            (node & 127).astype(f32),
            jnp.where(node_row >= half_nodes, 128.0, 0.0),
        ),
        map_lhs,
        map_hot,
    )
    rrow_m[...] = relay_maps[0:chips]
    rcol_m[...] = relay_maps[chips : 2 * chips]
    isend[:, 0, :] = relay_maps[2 * chips : 3 * chips]
    isend[:, 1, :] = relay_maps[3 * chips : 4 * chips] + relay_maps[4 * chips : 5 * chips]

    def relay_send(sb, rb, which, before):
        def post(t):
            for k in range(2):
                pltpu.make_async_remote_copy(
                    src_ref=sb.at[t],
                    dst_ref=rb.at[2 * t + core],
                    send_sem=send_sem.at[which],
                    recv_sem=recv_sem.at[which, 0],
                    device_id={"blocks": to_chip(t, k)},
                ).start()

        before(0)
        for t in range(2 * BATCH):
            post(t)
        before(BATCH)
        for t in range(2 * BATCH, last):
            post(t)
        pltpu.make_async_remote_copy(
            src_ref=sb.at[last],
            dst_ref=rb.at[2 * last + core],
            send_sem=send_sem.at[which],
            recv_sem=recv_sem.at[which, 0],
            device_id={"blocks": to_chip(last, 1 - core)},
        ).start()
        pltpu.make_async_copy(sb.at[last], rb.at[2 * last + core], recv_sem.at[which, 0]).start()

    relay_send(isend, irecv, SWEEPS, lambda u: None)

    def build_relay(u, carry):
        hot = jnp.where(fiota((LANES, WIDE), 0) == pair_at(rcol_m, u), 1.0, 0.0).astype(bf16)
        relay_hot[u, 0:LANES] = hot
        relay_hot[u, LANES:WIDE] = hot
        relay_mask[u] = jnp.where(fiota((qrows, WIDE), 0) + 1.0 == pair_at(rrow_m, u), 1.0, 0.0)
        return carry

    lax.fori_loop(0, chips // 2, build_relay, 0)
    update(receive(1))

    send_sweep(2)
    local_terms()
    loads[4].wait()
    for copy in halos0:
        copy.wait_recv()
    coef[...] = OMEGA / (6.0 + stiff[...])
    centre, beside = neighbours(0, mesh0)
    base[...] = (1.0 - OMEGA) * centre + coef[...][None] * beside

    wait_for(irecv, recv_sem.at[SWEEPS, 0])
    mine = iota((1, LANES), 1) // cap == core

    def build_nodes(u, carry):
        lanes = pl.ds(pl.multiple_of(u * WIDE, WIDE), WIDE)
        where = jnp.concatenate(
            [jnp.where(mine, irecv[4 * u + 2 * k], irecv[4 * u + 2 * k + 1]) for k in range(2)], axis=1
        )
        inode[u] = where
        node_hot[:, lanes] = jnp.where(fiota((WIDE, WIDE), 0) == where[1:2], 1.0, 0.0).astype(bf16)
        return carry

    lax.fori_loop(0, chips // 2, build_nodes, 0)
    update(receive(2))

    loads[5].wait()
    weight = oweight_ref[o]
    obj_copies = []
    for s in [n_obj // 2, *(s for s in range(1, n_obj) if s != n_obj // 2), 0]:
        q = lax.rem(o + s, n_obj)

        first = q * (qrows // 2)
        values = [gathered(surf_hot[first + k], surf_mask[first + k]) for k in range(qrows // 2)]
        for k, value in enumerate(values):
            lanes = pl.ds(pl.multiple_of((first + k) * WIDE, WIDE), WIDE)
            part = grad[0, :, lanes] * value[0:1]
            for f in range(1, fields):
                part = part + grad[f, :, lanes] * value[f : f + 1]
            part = part * weight
            ssend[s, 2 * k] = part[:, 0:LANES]
            ssend[s, 2 * k + 1] = part[:, LANES:WIDE]
        if s:
            copy = pltpu.make_async_remote_copy(
                src_ref=ssend.at[s],
                dst_ref=srecv.at[s - 1],
                send_sem=obj_send.at[s - 1],
                recv_sem=obj_recv.at[s - 1],
                device_id={"obj": q},
            )
            copy.start()
            obj_copies.append(copy)
    for copy in obj_copies:
        copy.wait_recv()
    comb[...] = ssend[0] + srecv[0] + srecv[1] + srecv[2]
    combined = jnp.concatenate([comb[:, c, :] for c in range(comps)], axis=0)
    high, low = halves(combined)
    vhl[:, 0:LANES] = high.astype(bf16)
    vhl[:, LANES:WIDE] = low.astype(bf16)

    def pick(first):
        values = []
        for u in range(first, first + BATCH):
            found = dot(vhl[...], relay_hot[u]).reshape(comps, qrows, WIDE)
            values.append(jnp.sum(found * relay_mask[u][None], axis=1))
        for u, value in enumerate(values, first):
            vsend[2 * u] = value[:, 0:LANES]
            vsend[2 * u + 1] = value[:, LANES:WIDE]

    relay_send(vsend, vrecv, SWEEPS + 1, pick)

    wait_for(vrecv, recv_sem.at[SWEEPS + 1, 0])

    def place_nodes(u):
        lanes = slice(u * WIDE, (u + 1) * WIDE)
        value = jnp.concatenate(
            [jnp.where(mine, vrecv[4 * u + 2 * k], vrecv[4 * u + 2 * k + 1]) for k in range(2)], axis=1
        )
        mask = fiota((half_nodes, WIDE), 0) == inode[u][0:1]
        for part, these in enumerate(halves(value)):
            for c in range(comps):
                at = (part * comps + c) * half_nodes
                node_lhs[at : at + half_nodes, lanes] = jnp.where(mask, these[c : c + 1], 0.0).astype(bf16)

    forces = None
    for u in range(0, chips // 2, CHAIN):
        for j in range(CHAIN):
            place_nodes(u + j)
        lanes = slice(u * WIDE, (u + CHAIN) * WIDE)
        part = dot_nt(node_lhs[:, lanes], node_hot[:, lanes])
        forces = part if forces is None else forces + part
    forces = forces[0 : comps * half_nodes] + forces[comps * half_nodes :]
    forces = forces.reshape(comps, size_x // 2, size_y, WIDE)
    force = jnp.concatenate([forces[..., 0:LANES], forces[..., LANES:WIDE]], axis=1)

    scaled = coef[...][None] * force
    first = base[...] + scaled
    mesh1[...] = first
    ysend[1, 0] = mesh1[:, :, size_y - 1, :]
    ysend[1, 1] = mesh1[:, :, 0, :]
    halos1 = halo_copies(1, mesh1)
    for copy in halos1:
        copy.start()
    for copy in halos1:
        copy.wait_recv()
    centre, beside = neighbours(1, mesh1)
    mesh2[...] = (1.0 - OMEGA) * centre + scaled + coef[...][None] * beside

    for copy in halos0 + halos1 + obj_copies:
        copy.wait_send()
    wait_for(sbuf0.at[pl.ds(0, n_blocks - 1)], send_sem.at[0])
    for sweep in range(1, SWEEPS):
        wait_for(sbuf1.at[sweep - 1, pl.ds(0, n_blocks - 1)], send_sem.at[sweep])
    for sb, which in ((irecv, SWEEPS), (vrecv, SWEEPS + 1)):
        wait_for(sb.at[pl.ds(0, n_blocks - 1)], send_sem.at[which])


def shards(
    n_blocks, n_obj, start, source, binv, coup, send, peer, recv, wgt, scell, grad, oweight, owner, node, mesh, stiff
):
    _, fields, rows_y, cols = start.shape
    faces, surf = send.shape[0], scell.shape[0]
    comps, size_x, size_y, _ = mesh.shape
    quarter = surf // n_obj
    qrows = quarter // LANES
    chips = n_blocks // 2
    half_nodes = size_x * size_y // 2
    vmem = pl.BlockSpec(memory_space=pltpu.VMEM)
    smem = pl.BlockSpec(memory_space=pltpu.SMEM)
    hbm = pl.BlockSpec(memory_space=pl.ANY)
    V = pltpu.VMEM
    dma = pltpu.SemaphoreType.DMA
    call = pl.pallas_call(
        functools.partial(kernel, n_blocks, n_obj, fields, rows_y, faces, surf, comps, size_x, size_y),
        out_shape=(
            V((fields * rows_y, cols), f32),
            V(mesh.shape, f32),
        ),
        in_specs=[hbm] * 10 + [smem] + [hbm] * 4,
        out_specs=(vmem, vmem),
        scratch_shapes=[
            V((fields, rows_y, cols), f32),
            V(binv.shape, f32),
            V(coup.shape, f32),
            V((fields, comps, surf), f32),
            V(mesh.shape, f32),
            V(stiff.shape, f32),
            V((faces // LANES, LANES), i32),
            V((faces // LANES, LANES), i32),
            V((faces // LANES, LANES), i32),
            V((faces // LANES, LANES), f32),
            V((fields, rows_y, cols), f32),
            V((surf // LANES, LANES), i32),
            V((qrows, LANES), i32),
            V((qrows, LANES), i32),
            V((faces // WIDE * n_blocks, 2 * WIDE), bf16),
            V((6 * chips, faces), bf16),
            V((WIDE, faces), bf16),
            V((chips, WIDE), f32),
            V((chips, WIDE), f32),
            V((chips, WIDE), f32),
            V((chips, WIDE, WIDE), bf16),
            V((chips, rows_y, WIDE), f32),
            V((surf // WIDE, WIDE, WIDE), bf16),
            V((surf // WIDE, rows_y, WIDE), f32),
            V((fields * rows_y, WIDE), bf16),
            V((fields, rows_y, LANES), f32),
            V((n_blocks, fields + 1, LANES), f32),
            V((n_blocks, fields + 1, LANES), f32),
            V((SWEEPS - 1, n_blocks, fields, LANES), f32),
            V((SWEEPS - 1, n_blocks, fields, LANES), f32),
            V((WIDE, chips * WIDE), bf16),
            V((fields * rows_y, chips * WIDE), bf16),
            V((n_obj, qrows, comps, LANES), f32),
            V((n_obj - 1, qrows, comps, LANES), f32),
            V((qrows, comps, LANES), f32),
            V((comps * qrows, WIDE), bf16),
            V((chips, 1, WIDE), i32),
            V((chips, LANES), f32),
            V((chips, LANES), f32),
            V((chips // 2, WIDE, WIDE), bf16),
            V((chips // 2, qrows, WIDE), f32),
            V((chips, 2, LANES), f32),
            V((n_blocks, 2, LANES), f32),
            V((chips, comps, LANES), f32),
            V((n_blocks, comps, LANES), f32),
            V((WIDE, chips * LANES), bf16),
            V((2 * comps * half_nodes, chips * LANES), bf16),
            V((chips // 2, 2, WIDE), f32),
            V(mesh.shape, f32),
            V(mesh.shape, f32),
            V(stiff.shape, f32),
            V((2, 2, comps, size_x, LANES), f32),
            V((2, 2, comps, size_x, LANES), f32),
            V((2, 2, comps, size_y, LANES), f32),
            dma((14,)),
            dma((SWEEPS + 2,)),
            dma((SWEEPS + 2, GROUPS)),
            dma((n_obj - 1,)),
            dma((n_obj - 1,)),
            dma((2, 4)),
            dma((2, 4)),
        ],
        compiler_params=pltpu.CompilerParams(
            collective_id=0, has_side_effects=True, vmem_limit_bytes=56 * 1024 * 1024
        ),
    )
    flow, mesh_adjoint = call(
        start[0],
        source[0],
        binv,
        coup,
        send.reshape(-1, LANES),
        peer.reshape(-1, LANES),
        recv.reshape(-1, LANES),
        wgt.reshape(-1, LANES),
        scell.reshape(-1, LANES),
        jnp.transpose(grad, (1, 0, 2)),
        oweight,
        owner.reshape(-1, LANES),
        node.reshape(-1, LANES),
        mesh,
        stiff,
    )
    return flow.reshape(start.shape), mesh_adjoint


def solution(mesh):
    placed = (
        P("obj", None, "blocks", None),
        P("obj", None, "blocks", None),
        P(None, None, "blocks", None),
        P(None, "blocks", None),
        P("blocks"),
        P("blocks", None),
        P("blocks"),
        P("blocks"),
        P("blocks"),
        P(None, None, "blocks"),
        P(),
        P(("blocks", "obj"), None),
        P(("blocks", "obj")),
        P(None, "blocks", "obj", None),
        P("blocks", "obj", None),
    )
    return jax.shard_map(
        functools.partial(shards, mesh.shape["blocks"], mesh.shape["obj"]),
        mesh=mesh,
        in_specs=placed,
        out_specs=(P("obj", None, "blocks", None), P(None, "blocks", "obj", None)),
        check_vma=False,
    )
```

```python
import functools

import jax
import jax.numpy as jnp
from jax import lax
from jax.experimental import pallas as pl
from jax.experimental.pallas import tpu as pltpu
from jax.sharding import PartitionSpec as P

OMEGA = 0.8
SWEEPS = 3
GROUPS = 4
BATCH = 8
CHAIN = 4
RING_Y = 4
POSTS = (0, 4, 8, 16, 24, 32)
TAKEN = ((0, 1), (2, 3))

f32, bf16, i32 = jnp.float32, jnp.bfloat16, jnp.int32
LANES = 128
WIDE = 256


def dot(a, b):
    return lax.dot_general(a, b, (((1,), (0,)), ((), ())), preferred_element_type=f32)


def dot_nt(a, b):
    return lax.dot_general(a, b, (((1,), (1,)), ((), ())), preferred_element_type=f32)


def iota(shape, dim):
    return lax.broadcasted_iota(i32, shape, dim)


def fiota(shape, dim):
    return iota(shape, dim).astype(f32)


def far_first(i, n):
    return (n // 2 + (1 - 2 * (i % 2)) * ((i + 1) // 2)) % n


def place_of(distance, n):
    d = distance - n // 2
    return jnp.where(d < 0, -2 * d - 1, 2 * d)


def halves(x):
    high = x.astype(bf16).astype(f32)
    return high, x - high


def pair(array, k):
    return jnp.concatenate([array[2 * k : 2 * k + 1], array[2 * k + 1 : 2 * k + 2]], axis=1)


def pair_at(ref, k):
    return jnp.concatenate([ref[pl.ds(2 * k, 1), :], ref[pl.ds(2 * k + 1, 1), :]], axis=1)


def bucket_ranks(bucket, chunks, buckets, lhs):
    before = jnp.zeros((buckets, WIDE), f32)
    ids = iota((buckets, WIDE), 0)
    a, b = iota((2 * WIDE, WIDE), 0), iota((2 * WIDE, WIDE), 1)
    upto = jnp.where((a <= b) | (a >= WIDE), 1.0, 0.0).astype(bf16)
    ranks = []
    for c in range(0, chunks, CHAIN):
        hots = []
        for g in range(c, c + CHAIN):
            hot = jnp.where(ids == pair(bucket, g), 1.0, 0.0)
            rows = slice(g * buckets, (g + 1) * buckets)
            lhs[rows, 0:WIDE] = hot.astype(bf16)
            lhs[rows, WIDE : 2 * WIDE] = before.astype(bf16)
            before = before + hot
            hots.append(hot)
        counts = dot(lhs[c * buckets : (c + CHAIN) * buckets, :], upto)
        for j, hot in enumerate(hots):
            ranks.append(jnp.sum(counts[j * buckets : (j + 1) * buckets] * hot, axis=0, keepdims=True) - 1.0)
    return ranks


def slot_maps(row_of, rows, ranks, width, values, lhs, hot_slot):
    ids = iota((rows, WIDE), 0)
    slots = fiota((width, WIDE), 0)
    high, total = len(values) * rows, None
    for c in range(0, len(ranks), CHAIN):
        for g in range(c, c + CHAIN):
            lanes = slice(g * WIDE, (g + 1) * WIDE)
            hot_slot[0:width, lanes] = jnp.where(slots == ranks[g], 1.0, 0.0).astype(bf16)
            mask = ids == pair(row_of, g)
            for j, value in enumerate(values):
                lhs[j * rows : (j + 1) * rows, lanes] = jnp.where(mask, pair(value, g), 0.0).astype(bf16)
        lanes = slice(c * WIDE, (c + CHAIN) * WIDE)
        part = dot_nt(lhs[0:high, lanes], hot_slot[0:width, lanes])
        total = part if total is None else total + part
    return total


def shifted(x, shift, axis):
    size = x.shape[axis]
    at = iota(x.shape, axis)
    edge = 0 if shift == 1 else size - 1
    return jnp.where(at == edge, 0.0, pltpu.roll(x, 1 if shift == 1 else size - 1, axis))


def kernel(
    n_blocks, n_obj, fields, rows_y, faces, surf, comps, size_x, size_y,
    start_hbm, source_hbm, binv_hbm, coup_hbm, send_hbm, peer_hbm, recv_hbm, wgt_hbm, scell_hbm, grad_hbm, oweight_ref,
    owner_hbm, node_hbm, mesh_hbm, stiff_hbm,
    lam, mesh2,
    source, binv, coup, grad, mesh0, stiff, peer_ref, send_ref, recv_ref, wgt_ref, start_ref, scell_ref, owner_ref, node_ref,
    rank_lhs, map_lhs, map_hot, scol_m, srow_m, wgt_m,
    chot, wmask, surf_hot, surf_mask, xhl, local,
    sbuf0, rbuf0, sbuf1, rbuf1, recv_hot, recv_lhs,
    ssend, srecv, comb, vhl,
    recv_row_m, rcol_m, rrow_m, relay_hot, relay_mask, isend, irecv, vsend, vrecv, node_hot, node_lhs, inode,
    mesh1, base, coef, ysend, yrecv, xrecv,
    in_sem, send_sem, recv_sem, obj_send, obj_recv, halo_send, halo_recv,
):
    b, o = lax.axis_index("blocks"), lax.axis_index("obj")
    chips = n_blocks // 2
    chip, core = b // 2, b % 2
    half_y = rows_y // 2
    group = chips // GROUPS
    quarter = surf // n_obj
    qrows = quarter // LANES

    ring_z = chips // RING_Y
    chip_z, chip_y = chip // RING_Y, chip % RING_Y
    last = chips - 1

    z_part = [lax.rem(chip_z + far_first(i, ring_z), ring_z) * (2 * RING_Y) for i in range(ring_z)]
    y_part = [lax.rem(chip_y + far_first(i, RING_Y), RING_Y) * 2 for i in range(RING_Y)]

    def to_chip(t, k):
        return z_part[t // RING_Y] + y_part[t % RING_Y] + k

    def slot_of(block):
        z = place_of(((block // (2 * RING_Y)) - chip_z) & (ring_z - 1), ring_z)
        y = place_of(((block // 2) - chip_y) & (RING_Y - 1), RING_Y)
        return (z * RING_Y + y) * 2 + (block & 1)

    barrier = pltpu.get_barrier_semaphore()
    for t in range(last):
        for k in range(2):
            pl.semaphore_signal(barrier, inc=1, device_id={"blocks": to_chip(t, k)})
    pl.semaphore_signal(barrier, inc=1, device_id={"blocks": to_chip(last, 1 - core)})
    for s in range(1, n_obj):
        pl.semaphore_signal(barrier, inc=1, device_id={"obj": lax.rem(o + s, n_obj)})

    loads = []
    for k, (src, dst) in enumerate(
        (
            (source_hbm, source), (coup_hbm, coup), (binv_hbm, binv), (mesh_hbm, mesh0), (stiff_hbm, stiff), (grad_hbm, grad),
            (peer_hbm, peer_ref), (send_hbm, send_ref), (recv_hbm, recv_ref), (wgt_hbm, wgt_ref), (start_hbm, start_ref),
            (scell_hbm, scell_ref), (owner_hbm, owner_ref), (node_hbm, node_ref),
        )
    ):
        loads.append(pltpu.make_async_copy(src, dst, in_sem.at[k]))
    for k in (*range(6, len(loads)), *range(6)):
        loads[k].start()


    for k in range(6, 10):
        loads[k].wait()

    peer = peer_ref[...]
    slot_row = slot_of(peer)
    ranks = bucket_ranks(slot_row, faces // WIDE, n_blocks, rank_lhs)
    send, recv, wgt = send_ref[...], recv_ref[...], wgt_ref[...]
    w_high, w_low = halves(wgt)
    side = (slot_row & 1) * LANES
    maps = slot_maps(
        slot_row >> 1,
        chips,
        [rank + pair(side, g).astype(f32) for g, rank in enumerate(ranks)],
        WIDE,
        (
            (send >> 7).astype(f32),
            (send & 127).astype(f32),
            w_high,
            w_low,
            (recv >> 7).astype(f32),
            (recv & 127).astype(f32),
        ),
        map_lhs,
        map_hot,
    )
    srow_m[...] = maps[0:chips]
    scol_m[...] = maps[chips : 2 * chips]
    wgt_m[...] = maps[2 * chips : 3 * chips] + maps[3 * chips : 4 * chips]
    target = maps[4 * chips : 5 * chips] * 128.0 + maps[5 * chips : 6 * chips]
    for t in range(chips):
        sbuf0[2 * t, fields:] = target[t : t + 1, 0:LANES]
        sbuf0[2 * t + 1, fields:] = target[t : t + 1, LANES:WIDE]

    def build(t, carry):
        hot = jnp.where(fiota((LANES, WIDE), 0) == scol_m[pl.ds(t, 1), :], 1.0, 0.0).astype(bf16)
        chot[t, 0:LANES] = hot
        chot[t, LANES:WIDE] = hot
        wmask[t] = jnp.where(fiota((rows_y, WIDE), 0) == srow_m[pl.ds(t, 1), :], wgt_m[pl.ds(t, 1), :], 0.0)
        return carry

    def set_lam(value):
        lam[...] = value
        high, low = halves(value)
        xhl[:, 0:LANES] = high.astype(bf16)
        xhl[:, LANES:WIDE] = low.astype(bf16)

    def gathered(hot, mask):
        found = dot(xhl[...], hot).reshape(fields, rows_y, WIDE)
        return jnp.sum(found * mask[None], axis=1)

    loads[10].wait()
    set_lam(start_ref[...].reshape(fields * rows_y, LANES))

    def send_sweep(sweep):
        sb, rb = (sbuf0, rbuf0) if sweep == 0 else (sbuf1.at[sweep - 1], rbuf1.at[sweep - 1])

        def fill(first, count):
            values = [gathered(chot[first + j], wmask[first + j]) for j in range(count)]
            for j, value in enumerate(values):
                sb[2 * (first + j), 0:fields] = value[:, 0:LANES]
                sb[2 * (first + j) + 1, 0:fields] = value[:, LANES:WIDE]

        def post(t, g):
            if t == last:
                pltpu.make_async_copy(sb.at[2 * t + core], rb.at[2 * t + core], recv_sem.at[sweep, g]).start()
            for k in [1 - core] if t == last else range(2):
                pltpu.make_async_remote_copy(
                    src_ref=sb.at[2 * t + k],
                    dst_ref=rb.at[2 * t + core],
                    send_sem=send_sem.at[sweep],
                    recv_sem=recv_sem.at[sweep, g],
                    device_id={"blocks": to_chip(t, k)},
                ).start()

        for first, end in zip(POSTS, POSTS[1:]):
            if sweep == 0:
                lax.fori_loop(first, end, build, 0)
            fill(first, end - first)
            if sweep == 0 and first == 0:
                pl.semaphore_wait(barrier, n_blocks - 1 + n_obj - 1)
            for t in range(first, end):
                post(t, t // group)

    def wait_for(ref, sem):
        pltpu.make_async_copy(ref, ref, sem).wait()

    def receive(sweep):
        rb = rbuf0 if sweep == 0 else rbuf1.at[sweep - 1]
        def place(t):
            lanes = slice(t * WIDE, (t + 1) * WIDE)
            first, second = rb[2 * t], rb[2 * t + 1]
            if sweep == 0:
                cell = jnp.concatenate([first[fields:], second[fields:]], axis=1).astype(i32)
                row = cell >> 7
                col = (cell & 127) + jnp.where(row >= half_y, LANES, 0)
                recv_row_m[t] = row & (half_y - 1)
                recv_hot[:, lanes] = jnp.where(iota((WIDE, WIDE), 0) == col, 1.0, 0.0).astype(bf16)
            mask = iota((half_y, WIDE), 0) == recv_row_m[t]
            value = jnp.concatenate([first[0:fields], second[0:fields]], axis=1)
            for part, these in enumerate(halves(value)):
                for f in range(fields):
                    at = (part * fields + f) * half_y
                    recv_lhs[at : at + half_y, lanes] = jnp.where(mask, these[f : f + 1], 0.0).astype(bf16)

        totals = [None, None]
        for groups in TAKEN:
            for g in groups:
                wait_for(rb.at[pl.ds(2 * group * g, 2 * group)], recv_sem.at[sweep, g])
            tiles = [t for g in groups for t in range(group * g, group * (g + 1), CHAIN)]
            for i, t in enumerate(tiles):
                for j in range(CHAIN):
                    place(t + j)
                lanes = slice(t * WIDE, (t + CHAIN) * WIDE)
                part = dot_nt(recv_lhs[:, lanes], recv_hot[:, lanes])
                totals[i % 2] = part if totals[i % 2] is None else totals[i % 2] + part
        total = totals[0] + totals[1]
        both = total[0 : fields * half_y] + total[fields * half_y :]
        face = []
        for f in range(fields):
            part = both[f * half_y : (f + 1) * half_y]
            face.append(jnp.concatenate([part[:, 0:LANES], part[:, LANES:WIDE]], axis=0))
        return face

    def update(face):
        rhs = [local[f] + face[f] for f in range(fields)]
        new = []
        for f in range(fields):
            acc = binv[f, 0] * rhs[0]
            for g in range(1, fields):
                acc = acc + binv[f, g] * rhs[g]
            new.append((1.0 - OMEGA) * lam[f * rows_y : (f + 1) * rows_y] + OMEGA * acc)
        set_lam(jnp.concatenate(new, axis=0))

    def local_terms():
        for f in range(fields):
            x = lam[f * rows_y : (f + 1) * rows_y]
            interior = coup[0] * shifted(x, 1, 0) + coup[1] * shifted(x, -1, 0)
            interior = interior + coup[2] * shifted(x, 1, 1) + coup[3] * shifted(x, -1, 1)
            local[f] = source[f] + interior

    ends = (lax.rem(b + 1, n_blocks), lax.rem(b + n_blocks - 1, n_blocks))
    sides = (lax.rem(o + 1, n_obj), lax.rem(o + n_obj - 1, n_obj))

    def halo_copies(sweep, field):
        copies = []
        for k in range(2):
            edge = size_x - 1 if k == 0 else 0
            copies.append(
                pltpu.make_async_remote_copy(
                    src_ref=field.at[:, edge],
                    dst_ref=xrecv.at[sweep, k],
                    send_sem=halo_send.at[sweep, k],
                    recv_sem=halo_recv.at[sweep, k],
                    device_id={"blocks": ends[k]},
                )
            )
            copies.append(
                pltpu.make_async_remote_copy(
                    src_ref=ysend.at[sweep, k],
                    dst_ref=yrecv.at[sweep, k],
                    send_sem=halo_send.at[sweep, 2 + k],
                    recv_sem=halo_recv.at[sweep, 2 + k],
                    device_id={"obj": sides[k]},
                )
            )
        return copies

    def neighbours(sweep, field):
        x = field[...]
        zero = jnp.zeros((comps, 1, size_y, LANES), f32)
        low = jnp.where(b > 0, xrecv[sweep, 0][:, None], zero)
        high = jnp.where(b < n_blocks - 1, xrecv[sweep, 1][:, None], zero)
        beside = jnp.concatenate([x[:, 1:], high], axis=1) + jnp.concatenate([low, x[:, :-1]], axis=1)
        flat = x.reshape(comps * size_x * size_y, LANES)
        total = flat.shape[0]
        at = iota((comps, size_x, size_y, LANES), 2)
        before = jnp.where(o > 0, yrecv[sweep, 0], 0.0)[:, :, None]
        after = jnp.where(o < n_obj - 1, yrecv[sweep, 1], 0.0)[:, :, None]
        up = pltpu.roll(flat, total - 1, 0).reshape(x.shape)
        down = pltpu.roll(flat, 1, 0).reshape(x.shape)
        beside = beside + jnp.where(at == size_y - 1, after, up) + jnp.where(at == 0, before, down)
        sideways = shifted(flat, -1, 1) + shifted(flat, 1, 1)
        return x, beside + sideways.reshape(x.shape)

    send_sweep(0)
    loads[3].wait()
    ysend[0, 0] = mesh0[:, :, size_y - 1, :]
    ysend[0, 1] = mesh0[:, :, 0, :]
    halos0 = halo_copies(0, mesh0)
    for copy in halos0:
        copy.start()
    loads[0].wait()
    loads[1].wait()
    local_terms()
    loads[2].wait()

    def build_surface(t, carry):
        cell = pair_at(scell_ref, t)
        hot = jnp.where(iota((LANES, WIDE), 0) == (cell & 127), 1.0, 0.0).astype(bf16)
        surf_hot[t, 0:LANES] = hot
        surf_hot[t, LANES:WIDE] = hot
        surf_mask[t] = jnp.where(iota((rows_y, WIDE), 0) == (cell >> 7), 1.0, 0.0)
        return carry

    loads[11].wait()
    lax.fori_loop(0, surf // WIDE, build_surface, 0)
    update(receive(0))

    send_sweep(1)
    local_terms()
    loads[12].wait()
    loads[13].wait()
    owner, node = owner_ref[...], node_ref[...]
    bucket = slot_of(owner)
    relay_ranks = bucket_ranks(bucket, quarter // WIDE, n_blocks, rank_lhs)
    cap = LANES // 2
    side = ((owner & 1) ^ core) * cap
    relay_ranks = [rank + pair(side, g).astype(f32) for g, rank in enumerate(relay_ranks)]
    node_row = node >> 7
    half_nodes = size_x * size_y // 2
    relay_maps = slot_maps(
        bucket >> 1,
        chips,
        relay_ranks,
        LANES,
        (
            fiota((qrows, LANES), 0) + 1.0,
            fiota((qrows, LANES), 1),
            (node_row & (half_nodes - 1)).astype(f32),
            (node & 127).astype(f32),
            jnp.where(node_row >= half_nodes, 128.0, 0.0),
        ),
        map_lhs,
        map_hot,
    )
    rrow_m[...] = relay_maps[0:chips]
    rcol_m[...] = relay_maps[chips : 2 * chips]
    isend[:, 0, :] = relay_maps[2 * chips : 3 * chips]
    isend[:, 1, :] = relay_maps[3 * chips : 4 * chips] + relay_maps[4 * chips : 5 * chips]

    def relay_send(sb, rb, which, before):
        def post(t):
            for k in range(2):
                pltpu.make_async_remote_copy(
                    src_ref=sb.at[t],
                    dst_ref=rb.at[2 * t + core],
                    send_sem=send_sem.at[which],
                    recv_sem=recv_sem.at[which, 2 * t // chips],
                    device_id={"blocks": to_chip(t, k)},
                ).start()

        before(0)
        for t in range(2 * BATCH):
            post(t)
        before(BATCH)
        for t in range(2 * BATCH, last):
            post(t)
        pltpu.make_async_remote_copy(
            src_ref=sb.at[last],
            dst_ref=rb.at[2 * last + core],
            send_sem=send_sem.at[which],
            recv_sem=recv_sem.at[which, 1],
            device_id={"blocks": to_chip(last, 1 - core)},
        ).start()
        pltpu.make_async_copy(sb.at[last], rb.at[2 * last + core], recv_sem.at[which, 1]).start()

    relay_send(isend, irecv, SWEEPS, lambda u: None)

    def build_relay(u, carry):
        hot = jnp.where(fiota((LANES, WIDE), 0) == pair_at(rcol_m, u), 1.0, 0.0).astype(bf16)
        relay_hot[u, 0:LANES] = hot
        relay_hot[u, LANES:WIDE] = hot
        relay_mask[u] = jnp.where(fiota((qrows, WIDE), 0) + 1.0 == pair_at(rrow_m, u), 1.0, 0.0)
        return carry

    lax.fori_loop(0, chips // 2, build_relay, 0)
    update(receive(1))

    send_sweep(2)
    local_terms()
    loads[4].wait()
    for copy in halos0:
        copy.wait_recv()
    coef[...] = OMEGA / (6.0 + stiff[...])
    centre, beside = neighbours(0, mesh0)
    base[...] = (1.0 - OMEGA) * centre + coef[...][None] * beside

    for h in range(2):
        wait_for(irecv.at[pl.ds(h * chips, chips)], recv_sem.at[SWEEPS, h])
    mine = iota((1, LANES), 1) // cap == core

    def build_nodes(u, carry):
        lanes = pl.ds(pl.multiple_of(u * WIDE, WIDE), WIDE)
        where = jnp.concatenate(
            [jnp.where(mine, irecv[4 * u + 2 * k], irecv[4 * u + 2 * k + 1]) for k in range(2)], axis=1
        )
        inode[u] = where
        node_hot[:, lanes] = jnp.where(fiota((WIDE, WIDE), 0) == where[1:2], 1.0, 0.0).astype(bf16)
        return carry

    lax.fori_loop(0, chips // 2, build_nodes, 0)
    update(receive(2))

    loads[5].wait()
    weight = oweight_ref[o]
    obj_copies = []
    for s in [n_obj // 2, *(s for s in range(1, n_obj) if s != n_obj // 2), 0]:
        q = lax.rem(o + s, n_obj)

        first = q * (qrows // 2)
        values = [gathered(surf_hot[first + k], surf_mask[first + k]) for k in range(qrows // 2)]
        for k, value in enumerate(values):
            lanes = pl.ds(pl.multiple_of((first + k) * WIDE, WIDE), WIDE)
            part = grad[0, :, lanes] * value[0:1]
            for f in range(1, fields):
                part = part + grad[f, :, lanes] * value[f : f + 1]
            part = part * weight
            ssend[s, 2 * k] = part[:, 0:LANES]
            ssend[s, 2 * k + 1] = part[:, LANES:WIDE]
        if s:
            copy = pltpu.make_async_remote_copy(
                src_ref=ssend.at[s],
                dst_ref=srecv.at[s - 1],
                send_sem=obj_send.at[s - 1],
                recv_sem=obj_recv.at[s - 1],
                device_id={"obj": q},
            )
            copy.start()
            obj_copies.append(copy)
    for copy in obj_copies:
        copy.wait_recv()
    comb[...] = ssend[0] + srecv[0] + srecv[1] + srecv[2]
    combined = jnp.concatenate([comb[:, c, :] for c in range(comps)], axis=0)
    high, low = halves(combined)
    vhl[:, 0:LANES] = high.astype(bf16)
    vhl[:, LANES:WIDE] = low.astype(bf16)

    def pick(first):
        values = []
        for u in range(first, first + BATCH):
            found = dot(vhl[...], relay_hot[u]).reshape(comps, qrows, WIDE)
            values.append(jnp.sum(found * relay_mask[u][None], axis=1))
        for u, value in enumerate(values, first):
            vsend[2 * u] = value[:, 0:LANES]
            vsend[2 * u + 1] = value[:, LANES:WIDE]

    relay_send(vsend, vrecv, SWEEPS + 1, pick)

    def place_nodes(u):
        lanes = slice(u * WIDE, (u + 1) * WIDE)
        value = jnp.concatenate(
            [jnp.where(mine, vrecv[4 * u + 2 * k], vrecv[4 * u + 2 * k + 1]) for k in range(2)], axis=1
        )
        mask = fiota((half_nodes, WIDE), 0) == inode[u][0:1]
        for part, these in enumerate(halves(value)):
            for c in range(comps):
                at = (part * comps + c) * half_nodes
                node_lhs[at : at + half_nodes, lanes] = jnp.where(mask, these[c : c + 1], 0.0).astype(bf16)

    forces = None
    for h in (1, 0):
        wait_for(vrecv.at[pl.ds(h * chips, chips)], recv_sem.at[SWEEPS + 1, h])
        for u in range(h * chips // 4, (h + 1) * chips // 4, CHAIN):
            for j in range(CHAIN):
                place_nodes(u + j)
            lanes = slice(u * WIDE, (u + CHAIN) * WIDE)
            part = dot_nt(node_lhs[:, lanes], node_hot[:, lanes])
            forces = part if forces is None else forces + part
    forces = forces[0 : comps * half_nodes] + forces[comps * half_nodes :]
    forces = forces.reshape(comps, size_x // 2, size_y, WIDE)
    force = jnp.concatenate([forces[..., 0:LANES], forces[..., LANES:WIDE]], axis=1)

    scaled = coef[...][None] * force
    first = base[...] + scaled
    mesh1[...] = first
    ysend[1, 0] = mesh1[:, :, size_y - 1, :]
    ysend[1, 1] = mesh1[:, :, 0, :]
    halos1 = halo_copies(1, mesh1)
    for copy in halos1:
        copy.start()
    for copy in halos1:
        copy.wait_recv()
    centre, beside = neighbours(1, mesh1)
    mesh2[...] = (1.0 - OMEGA) * centre + scaled + coef[...][None] * beside

    for copy in halos0 + halos1 + obj_copies:
        copy.wait_send()
    wait_for(sbuf0.at[pl.ds(0, n_blocks - 1)], send_sem.at[0])
    for sweep in range(1, SWEEPS):
        wait_for(sbuf1.at[sweep - 1, pl.ds(0, n_blocks - 1)], send_sem.at[sweep])
    for sb, which in ((irecv, SWEEPS), (vrecv, SWEEPS + 1)):
        wait_for(sb.at[pl.ds(0, n_blocks - 1)], send_sem.at[which])


def write_out(flow, mesh, flow_out, mesh_out, sems):
    copies = [pltpu.make_async_copy(flow, flow_out, sems.at[0]), pltpu.make_async_copy(mesh, mesh_out, sems.at[1])]
    for copy in copies:
        copy.start()
    for copy in copies:
        copy.wait()


def shards(
    n_blocks, n_obj, start, source, binv, coup, send, peer, recv, wgt, scell, grad, oweight, owner, node, mesh, stiff
):
    _, fields, rows_y, cols = start.shape
    faces, surf = send.shape[0], scell.shape[0]
    comps, size_x, size_y, _ = mesh.shape
    quarter = surf // n_obj
    qrows = quarter // LANES
    chips = n_blocks // 2
    half_nodes = size_x * size_y // 2
    vmem = pl.BlockSpec(memory_space=pltpu.VMEM)
    smem = pl.BlockSpec(memory_space=pltpu.SMEM)
    hbm = pl.BlockSpec(memory_space=pl.ANY)
    V = pltpu.VMEM
    dma = pltpu.SemaphoreType.DMA
    call = pl.pallas_call(
        functools.partial(kernel, n_blocks, n_obj, fields, rows_y, faces, surf, comps, size_x, size_y),
        out_shape=(
            V((fields * rows_y, cols), f32),
            V(mesh.shape, f32),
        ),
        in_specs=[hbm] * 10 + [smem] + [hbm] * 4,
        out_specs=(vmem, vmem),
        scratch_shapes=[
            V((fields, rows_y, cols), f32),
            V(binv.shape, f32),
            V(coup.shape, f32),
            V((fields, comps, surf), f32),
            V(mesh.shape, f32),
            V(stiff.shape, f32),
            V((faces // LANES, LANES), i32),
            V((faces // LANES, LANES), i32),
            V((faces // LANES, LANES), i32),
            V((faces // LANES, LANES), f32),
            V((fields, rows_y, cols), f32),
            V((surf // LANES, LANES), i32),
            V((qrows, LANES), i32),
            V((qrows, LANES), i32),
            V((faces // WIDE * n_blocks, 2 * WIDE), bf16),
            V((6 * chips, faces), bf16),
            V((WIDE, faces), bf16),
            V((chips, WIDE), f32),
            V((chips, WIDE), f32),
            V((chips, WIDE), f32),
            V((chips, WIDE, WIDE), bf16),
            V((chips, rows_y, WIDE), f32),
            V((surf // WIDE, WIDE, WIDE), bf16),
            V((surf // WIDE, rows_y, WIDE), f32),
            V((fields * rows_y, WIDE), bf16),
            V((fields, rows_y, LANES), f32),
            V((n_blocks, fields + 1, LANES), f32),
            V((n_blocks, fields + 1, LANES), f32),
            V((SWEEPS - 1, n_blocks, fields, LANES), f32),
            V((SWEEPS - 1, n_blocks, fields, LANES), f32),
            V((WIDE, chips * WIDE), bf16),
            V((fields * rows_y, chips * WIDE), bf16),
            V((n_obj, qrows, comps, LANES), f32),
            V((n_obj - 1, qrows, comps, LANES), f32),
            V((qrows, comps, LANES), f32),
            V((comps * qrows, WIDE), bf16),
            V((chips, 1, WIDE), i32),
            V((chips, LANES), f32),
            V((chips, LANES), f32),
            V((chips // 2, WIDE, WIDE), bf16),
            V((chips // 2, qrows, WIDE), f32),
            V((chips, 2, LANES), f32),
            V((n_blocks, 2, LANES), f32),
            V((chips, comps, LANES), f32),
            V((n_blocks, comps, LANES), f32),
            V((WIDE, chips * LANES), bf16),
            V((2 * comps * half_nodes, chips * LANES), bf16),
            V((chips // 2, 2, WIDE), f32),
            V(mesh.shape, f32),
            V(mesh.shape, f32),
            V(stiff.shape, f32),
            V((2, 2, comps, size_x, LANES), f32),
            V((2, 2, comps, size_x, LANES), f32),
            V((2, 2, comps, size_y, LANES), f32),
            dma((14,)),
            dma((SWEEPS + 2,)),
            dma((SWEEPS + 2, GROUPS)),
            dma((n_obj - 1,)),
            dma((n_obj - 1,)),
            dma((2, 4)),
            dma((2, 4)),
        ],
        compiler_params=pltpu.CompilerParams(
            collective_id=0, has_side_effects=True, vmem_limit_bytes=56 * 1024 * 1024
        ),
    )
    flow, mesh_adjoint = call(
        start[0],
        source[0],
        binv,
        coup,
        send.reshape(-1, LANES),
        peer.reshape(-1, LANES),
        recv.reshape(-1, LANES),
        wgt.reshape(-1, LANES),
        scell.reshape(-1, LANES),
        jnp.transpose(grad, (1, 0, 2)),
        oweight,
        owner.reshape(-1, LANES),
        node.reshape(-1, LANES),
        mesh,
        stiff,
    )
    flow, mesh_adjoint = pl.pallas_call(
        write_out,
        out_shape=(jax.ShapeDtypeStruct(flow.shape, f32), jax.ShapeDtypeStruct(mesh.shape, f32)),
        in_specs=[vmem, vmem],
        out_specs=(hbm, hbm),
        scratch_shapes=[dma((2,))],
    )(
        pltpu.with_memory_space_constraint(flow, pltpu.VMEM),
        pltpu.with_memory_space_constraint(mesh_adjoint, pltpu.VMEM),
    )
    return flow.reshape(start.shape), mesh_adjoint


def solution(mesh):
    placed = (
        P("obj", None, "blocks", None),
        P("obj", None, "blocks", None),
        P(None, None, "blocks", None),
        P(None, "blocks", None),
        P("blocks"),
        P("blocks", None),
        P("blocks"),
        P("blocks"),
        P("blocks"),
        P(None, None, "blocks"),
        P(),
        P(("blocks", "obj"), None),
        P(("blocks", "obj")),
        P(None, "blocks", "obj", None),
        P("blocks", "obj", None),
    )
    return jax.shard_map(
        functools.partial(shards, mesh.shape["blocks"], mesh.shape["obj"]),
        mesh=mesh,
        in_specs=placed,
        out_specs=(P("obj", None, "blocks", None), P(None, "blocks", "obj", None)),
        check_vma=False,
    )
```

```python
import functools

import jax
import jax.numpy as jnp
from jax import lax
from jax.experimental import pallas as pl
from jax.experimental.pallas import tpu as pltpu
from jax.sharding import PartitionSpec as P

OMEGA = 0.8
SWEEPS = 3
GROUPS = 4
BATCH = 8
CHAIN = 2
RING_Y = 4
POSTS = (0, 4, 8, 16, 24, 32)
TAKEN = ((0, 1), (2, 3))

f32, bf16, i32 = jnp.float32, jnp.bfloat16, jnp.int32
LANES = 128
WIDE = 256


def dot(a, b):
    return lax.dot_general(a, b, (((1,), (0,)), ((), ())), preferred_element_type=f32)


def dot_nt(a, b):
    return lax.dot_general(a, b, (((1,), (1,)), ((), ())), preferred_element_type=f32)


def iota(shape, dim):
    return lax.broadcasted_iota(i32, shape, dim)


def fiota(shape, dim):
    return iota(shape, dim).astype(f32)


def far_first(i, n):
    return (n // 2 + (1 - 2 * (i % 2)) * ((i + 1) // 2)) % n


def place_of(distance, n):
    d = distance - n // 2
    return jnp.where(d < 0, -2 * d - 1, 2 * d)


def halves(x):
    high = x.astype(bf16).astype(f32)
    return high, x - high


def pair(array, k):
    return jnp.concatenate([array[2 * k : 2 * k + 1], array[2 * k + 1 : 2 * k + 2]], axis=1)


def pair_at(ref, k):
    return jnp.concatenate([ref[pl.ds(2 * k, 1), :], ref[pl.ds(2 * k + 1, 1), :]], axis=1)


def bucket_ranks(bucket, chunks, buckets, lhs):
    before = jnp.zeros((buckets, WIDE), f32)
    ids = iota((buckets, WIDE), 0)
    a, b = iota((2 * WIDE, WIDE), 0), iota((2 * WIDE, WIDE), 1)
    upto = jnp.where((a <= b) | (a >= WIDE), 1.0, 0.0).astype(bf16)
    ranks = []
    for c in range(0, chunks, CHAIN):
        hots = []
        for g in range(c, c + CHAIN):
            hot = jnp.where(ids == pair(bucket, g), 1.0, 0.0)
            rows = slice(g * buckets, (g + 1) * buckets)
            lhs[rows, 0:WIDE] = hot.astype(bf16)
            lhs[rows, WIDE : 2 * WIDE] = before.astype(bf16)
            before = before + hot
            hots.append(hot)
        counts = dot(lhs[c * buckets : (c + CHAIN) * buckets, :], upto)
        for j, hot in enumerate(hots):
            ranks.append(jnp.sum(counts[j * buckets : (j + 1) * buckets] * hot, axis=0, keepdims=True) - 1.0)
    return ranks


def slot_maps(row_of, rows, ranks, width, values, lhs, hot_slot):
    ids = iota((rows, WIDE), 0)
    slots = fiota((width, WIDE), 0)
    high, total = len(values) * rows, None
    for c in range(0, len(ranks), CHAIN):
        for g in range(c, c + CHAIN):
            lanes = slice(g * WIDE, (g + 1) * WIDE)
            hot_slot[0:width, lanes] = jnp.where(slots == ranks[g], 1.0, 0.0).astype(bf16)
            mask = ids == pair(row_of, g)
            for j, value in enumerate(values):
                lhs[j * rows : (j + 1) * rows, lanes] = jnp.where(mask, pair(value, g), 0.0).astype(bf16)
        lanes = slice(c * WIDE, (c + CHAIN) * WIDE)
        part = dot_nt(lhs[0:high, lanes], hot_slot[0:width, lanes])
        total = part if total is None else total + part
    return total


def shifted(x, shift, axis):
    size = x.shape[axis]
    at = iota(x.shape, axis)
    edge = 0 if shift == 1 else size - 1
    return jnp.where(at == edge, 0.0, pltpu.roll(x, 1 if shift == 1 else size - 1, axis))


def kernel(
    n_blocks, n_obj, fields, rows_y, faces, surf, comps, size_x, size_y,
    start_hbm, source_hbm, binv_hbm, coup_hbm, send_hbm, peer_hbm, recv_hbm, wgt_hbm, scell_hbm, grad_hbm, oweight_ref,
    owner_hbm, node_hbm, mesh_hbm, stiff_hbm,
    lam, mesh2,
    source, binv, coup, grad, mesh0, stiff, peer_ref, send_ref, recv_ref, wgt_ref, start_ref, scell_ref, owner_ref, node_ref,
    rank_lhs, map_lhs, map_hot, scol_m, srow_m, wgt_m,
    chot, wmask, surf_hot, surf_mask, xhl, local,
    sbuf0, rbuf0, sbuf1, rbuf1, recv_hot, recv_lhs,
    ssend, srecv, comb, vhl,
    recv_row_m, rcol_m, rrow_m, relay_hot, relay_mask, isend, irecv, vsend, vrecv, node_hot, node_lhs, inode,
    mesh1, base, coef, ysend, yrecv, xrecv,
    in_sem, send_sem, recv_sem, obj_send, obj_recv, halo_send, halo_recv,
):
    b, o = lax.axis_index("blocks"), lax.axis_index("obj")
    chips = n_blocks // 2
    chip, core = b // 2, b % 2
    half_y = rows_y // 2
    group = chips // GROUPS
    quarter = surf // n_obj
    qrows = quarter // LANES

    ring_z = chips // RING_Y
    chip_z, chip_y = chip // RING_Y, chip % RING_Y
    last = chips - 1

    z_part = [lax.rem(chip_z + far_first(i, ring_z), ring_z) * (2 * RING_Y) for i in range(ring_z)]
    y_part = [lax.rem(chip_y + far_first(i, RING_Y), RING_Y) * 2 for i in range(RING_Y)]

    def to_chip(t, k):
        return z_part[t // RING_Y] + y_part[t % RING_Y] + k

    def slot_of(block):
        z = place_of(((block // (2 * RING_Y)) - chip_z) & (ring_z - 1), ring_z)
        y = place_of(((block // 2) - chip_y) & (RING_Y - 1), RING_Y)
        return (z * RING_Y + y) * 2 + (block & 1)

    barrier = pltpu.get_barrier_semaphore()
    for t in range(last):
        for k in range(2):
            pl.semaphore_signal(barrier, inc=1, device_id={"blocks": to_chip(t, k)})
    pl.semaphore_signal(barrier, inc=1, device_id={"blocks": to_chip(last, 1 - core)})
    for s in range(1, n_obj):
        pl.semaphore_signal(barrier, inc=1, device_id={"obj": lax.rem(o + s, n_obj)})

    loads = []
    for k, (src, dst) in enumerate(
        (
            (source_hbm, source), (coup_hbm, coup), (binv_hbm, binv), (mesh_hbm, mesh0), (stiff_hbm, stiff), (grad_hbm, grad),
            (peer_hbm, peer_ref), (send_hbm, send_ref), (recv_hbm, recv_ref), (wgt_hbm, wgt_ref), (start_hbm, start_ref),
            (scell_hbm, scell_ref), (owner_hbm, owner_ref), (node_hbm, node_ref),
        )
    ):
        loads.append(pltpu.make_async_copy(src, dst, in_sem.at[k]))
    for k in (*range(6, len(loads)), *range(6)):
        loads[k].start()


    for k in range(6, 10):
        loads[k].wait()

    peer = peer_ref[...]
    slot_row = slot_of(peer)
    ranks = bucket_ranks(slot_row, faces // WIDE, n_blocks, rank_lhs)
    send, recv, wgt = send_ref[...], recv_ref[...], wgt_ref[...]
    w_high, w_low = halves(wgt)
    side = (slot_row & 1) * LANES
    maps = slot_maps(
        slot_row >> 1,
        chips,
        [rank + pair(side, g).astype(f32) for g, rank in enumerate(ranks)],
        WIDE,
        (
            (send >> 7).astype(f32),
            (send & 127).astype(f32),
            w_high,
            w_low,
            (recv >> 7).astype(f32),
            (recv & 127).astype(f32),
        ),
        map_lhs,
        map_hot,
    )
    srow_m[...] = maps[0:chips]
    scol_m[...] = maps[chips : 2 * chips]
    wgt_m[...] = maps[2 * chips : 3 * chips] + maps[3 * chips : 4 * chips]
    target = maps[4 * chips : 5 * chips] * 128.0 + maps[5 * chips : 6 * chips]
    for t in range(chips):
        sbuf0[2 * t, fields:] = target[t : t + 1, 0:LANES]
        sbuf0[2 * t + 1, fields:] = target[t : t + 1, LANES:WIDE]

    def build(t, carry):
        hot = jnp.where(fiota((LANES, WIDE), 0) == scol_m[pl.ds(t, 1), :], 1.0, 0.0).astype(bf16)
        chot[t, 0:LANES] = hot
        chot[t, LANES:WIDE] = hot
        wmask[t] = jnp.where(fiota((rows_y, WIDE), 0) == srow_m[pl.ds(t, 1), :], wgt_m[pl.ds(t, 1), :], 0.0)
        return carry

    def set_lam(value):
        lam[...] = value
        high, low = halves(value)
        xhl[:, 0:LANES] = high.astype(bf16)
        xhl[:, LANES:WIDE] = low.astype(bf16)

    def gathered(hot, mask):
        found = dot(xhl[...], hot).reshape(fields, rows_y, WIDE)
        return jnp.sum(found * mask[None], axis=1)

    loads[10].wait()
    set_lam(start_ref[...].reshape(fields * rows_y, LANES))

    def send_sweep(sweep):
        sb, rb = (sbuf0, rbuf0) if sweep == 0 else (sbuf1.at[sweep - 1], rbuf1.at[sweep - 1])

        def fill(first, count):
            values = [gathered(chot[first + j], wmask[first + j]) for j in range(count)]
            for j, value in enumerate(values):
                sb[2 * (first + j), 0:fields] = value[:, 0:LANES]
                sb[2 * (first + j) + 1, 0:fields] = value[:, LANES:WIDE]

        def post(t, g):
            if t == last:
                pltpu.make_async_copy(sb.at[2 * t + core], rb.at[2 * t + core], recv_sem.at[sweep, g]).start()
            for k in [1 - core] if t == last else range(2):
                pltpu.make_async_remote_copy(
                    src_ref=sb.at[2 * t + k],
                    dst_ref=rb.at[2 * t + core],
                    send_sem=send_sem.at[sweep],
                    recv_sem=recv_sem.at[sweep, g],
                    device_id={"blocks": to_chip(t, k)},
                ).start()

        for first, end in zip(POSTS, POSTS[1:]):
            if sweep == 0:
                lax.fori_loop(first, end, build, 0)
            fill(first, end - first)
            if sweep == 0 and first == 0:
                pl.semaphore_wait(barrier, n_blocks - 1 + n_obj - 1)
            for t in range(first, end):
                post(t, t // group)

    def wait_for(ref, sem):
        pltpu.make_async_copy(ref, ref, sem).wait()

    def receive(sweep):
        rb = rbuf0 if sweep == 0 else rbuf1.at[sweep - 1]
        def place(t):
            lanes = slice(t * WIDE, (t + 1) * WIDE)
            first, second = rb[2 * t], rb[2 * t + 1]
            if sweep == 0:
                cell = jnp.concatenate([first[fields:], second[fields:]], axis=1).astype(i32)
                row = cell >> 7
                col = (cell & 127) + jnp.where(row >= half_y, LANES, 0)
                recv_row_m[t] = row & (half_y - 1)
                recv_hot[:, lanes] = jnp.where(iota((WIDE, WIDE), 0) == col, 1.0, 0.0).astype(bf16)
            mask = iota((half_y, WIDE), 0) == recv_row_m[t]
            value = jnp.concatenate([first[0:fields], second[0:fields]], axis=1)
            for part, these in enumerate(halves(value)):
                for f in range(fields):
                    at = (part * fields + f) * half_y
                    recv_lhs[at : at + half_y, lanes] = jnp.where(mask, these[f : f + 1], 0.0).astype(bf16)

        totals = [None, None]
        for groups in TAKEN:
            for g in groups:
                wait_for(rb.at[pl.ds(2 * group * g, 2 * group)], recv_sem.at[sweep, g])
            tiles = [t for g in groups for t in range(group * g, group * (g + 1), CHAIN)]
            for i, t in enumerate(tiles):
                for j in range(CHAIN):
                    place(t + j)
                lanes = slice(t * WIDE, (t + CHAIN) * WIDE)
                part = dot_nt(recv_lhs[:, lanes], recv_hot[:, lanes])
                totals[i % 2] = part if totals[i % 2] is None else totals[i % 2] + part
        total = totals[0] + totals[1]
        both = total[0 : fields * half_y] + total[fields * half_y :]
        face = []
        for f in range(fields):
            part = both[f * half_y : (f + 1) * half_y]
            face.append(jnp.concatenate([part[:, 0:LANES], part[:, LANES:WIDE]], axis=0))
        return face

    def update(face):
        rhs = [local[f] + face[f] for f in range(fields)]
        new = []
        for f in range(fields):
            acc = binv[f, 0] * rhs[0]
            for g in range(1, fields):
                acc = acc + binv[f, g] * rhs[g]
            new.append((1.0 - OMEGA) * lam[f * rows_y : (f + 1) * rows_y] + OMEGA * acc)
        set_lam(jnp.concatenate(new, axis=0))

    def local_terms():
        for f in range(fields):
            x = lam[f * rows_y : (f + 1) * rows_y]
            interior = coup[0] * shifted(x, 1, 0) + coup[1] * shifted(x, -1, 0)
            interior = interior + coup[2] * shifted(x, 1, 1) + coup[3] * shifted(x, -1, 1)
            local[f] = source[f] + interior

    ends = (lax.rem(b + 1, n_blocks), lax.rem(b + n_blocks - 1, n_blocks))
    sides = (lax.rem(o + 1, n_obj), lax.rem(o + n_obj - 1, n_obj))

    def halo_copies(sweep, field):
        copies = []
        for k in range(2):
            edge = size_x - 1 if k == 0 else 0
            copies.append(
                pltpu.make_async_remote_copy(
                    src_ref=field.at[:, edge],
                    dst_ref=xrecv.at[sweep, k],
                    send_sem=halo_send.at[sweep, k],
                    recv_sem=halo_recv.at[sweep, k],
                    device_id={"blocks": ends[k]},
                )
            )
            copies.append(
                pltpu.make_async_remote_copy(
                    src_ref=ysend.at[sweep, k],
                    dst_ref=yrecv.at[sweep, k],
                    send_sem=halo_send.at[sweep, 2 + k],
                    recv_sem=halo_recv.at[sweep, 2 + k],
                    device_id={"obj": sides[k]},
                )
            )
        return copies

    def neighbours(sweep, field):
        x = field[...]
        zero = jnp.zeros((comps, 1, size_y, LANES), f32)
        low = jnp.where(b > 0, xrecv[sweep, 0][:, None], zero)
        high = jnp.where(b < n_blocks - 1, xrecv[sweep, 1][:, None], zero)
        beside = jnp.concatenate([x[:, 1:], high], axis=1) + jnp.concatenate([low, x[:, :-1]], axis=1)
        flat = x.reshape(comps * size_x * size_y, LANES)
        total = flat.shape[0]
        at = iota((comps, size_x, size_y, LANES), 2)
        before = jnp.where(o > 0, yrecv[sweep, 0], 0.0)[:, :, None]
        after = jnp.where(o < n_obj - 1, yrecv[sweep, 1], 0.0)[:, :, None]
        up = pltpu.roll(flat, total - 1, 0).reshape(x.shape)
        down = pltpu.roll(flat, 1, 0).reshape(x.shape)
        beside = beside + jnp.where(at == size_y - 1, after, up) + jnp.where(at == 0, before, down)
        sideways = shifted(flat, -1, 1) + shifted(flat, 1, 1)
        return x, beside + sideways.reshape(x.shape)

    send_sweep(0)
    loads[3].wait()
    ysend[0, 0] = mesh0[:, :, size_y - 1, :]
    ysend[0, 1] = mesh0[:, :, 0, :]
    halos0 = halo_copies(0, mesh0)
    for copy in halos0:
        copy.start()
    loads[0].wait()
    loads[1].wait()
    local_terms()
    loads[2].wait()

    def build_surface(t, carry):
        cell = pair_at(scell_ref, t)
        hot = jnp.where(iota((LANES, WIDE), 0) == (cell & 127), 1.0, 0.0).astype(bf16)
        surf_hot[t, 0:LANES] = hot
        surf_hot[t, LANES:WIDE] = hot
        surf_mask[t] = jnp.where(iota((rows_y, WIDE), 0) == (cell >> 7), 1.0, 0.0)
        return carry

    loads[11].wait()
    lax.fori_loop(0, surf // WIDE, build_surface, 0)
    update(receive(0))

    send_sweep(1)
    local_terms()
    loads[12].wait()
    loads[13].wait()
    owner, node = owner_ref[...], node_ref[...]
    bucket = slot_of(owner)
    relay_ranks = bucket_ranks(bucket, quarter // WIDE, n_blocks, rank_lhs)
    cap = LANES // 2
    side = ((owner & 1) ^ core) * cap
    relay_ranks = [rank + pair(side, g).astype(f32) for g, rank in enumerate(relay_ranks)]
    node_row = node >> 7
    half_nodes = size_x * size_y // 2
    relay_maps = slot_maps(
        bucket >> 1,
        chips,
        relay_ranks,
        LANES,
        (
            fiota((qrows, LANES), 0) + 1.0,
            fiota((qrows, LANES), 1),
            (node_row & (half_nodes - 1)).astype(f32),
            (node & 127).astype(f32),
            jnp.where(node_row >= half_nodes, 128.0, 0.0),
        ),
        map_lhs,
        map_hot,
    )
    rrow_m[...] = relay_maps[0:chips]
    rcol_m[...] = relay_maps[chips : 2 * chips]
    isend[:, 0, :] = relay_maps[2 * chips : 3 * chips]
    isend[:, 1, :] = relay_maps[3 * chips : 4 * chips] + relay_maps[4 * chips : 5 * chips]

    def relay_send(sb, rb, which, before):
        def post(t):
            for k in range(2):
                pltpu.make_async_remote_copy(
                    src_ref=sb.at[t],
                    dst_ref=rb.at[2 * t + core],
                    send_sem=send_sem.at[which],
                    recv_sem=recv_sem.at[which, 2 * t // chips],
                    device_id={"blocks": to_chip(t, k)},
                ).start()

        before(0)
        for t in range(2 * BATCH):
            post(t)
        before(BATCH)
        for t in range(2 * BATCH, last):
            post(t)
        pltpu.make_async_remote_copy(
            src_ref=sb.at[last],
            dst_ref=rb.at[2 * last + core],
            send_sem=send_sem.at[which],
            recv_sem=recv_sem.at[which, 1],
            device_id={"blocks": to_chip(last, 1 - core)},
        ).start()
        pltpu.make_async_copy(sb.at[last], rb.at[2 * last + core], recv_sem.at[which, 1]).start()

    relay_send(isend, irecv, SWEEPS, lambda u: None)

    def build_relay(u, carry):
        hot = jnp.where(fiota((LANES, WIDE), 0) == pair_at(rcol_m, u), 1.0, 0.0).astype(bf16)
        relay_hot[u, 0:LANES] = hot
        relay_hot[u, LANES:WIDE] = hot
        relay_mask[u] = jnp.where(fiota((qrows, WIDE), 0) + 1.0 == pair_at(rrow_m, u), 1.0, 0.0)
        return carry

    lax.fori_loop(0, chips // 2, build_relay, 0)
    update(receive(1))

    send_sweep(2)
    local_terms()
    loads[4].wait()
    for copy in halos0:
        copy.wait_recv()
    coef[...] = OMEGA / (6.0 + stiff[...])
    centre, beside = neighbours(0, mesh0)
    base[...] = (1.0 - OMEGA) * centre + coef[...][None] * beside

    for h in range(2):
        wait_for(irecv.at[pl.ds(h * chips, chips)], recv_sem.at[SWEEPS, h])
    mine = iota((1, LANES), 1) // cap == core

    def build_nodes(u, carry):
        lanes = pl.ds(pl.multiple_of(u * WIDE, WIDE), WIDE)
        where = jnp.concatenate(
            [jnp.where(mine, irecv[4 * u + 2 * k], irecv[4 * u + 2 * k + 1]) for k in range(2)], axis=1
        )
        inode[u] = where
        node_hot[:, lanes] = jnp.where(fiota((WIDE, WIDE), 0) == where[1:2], 1.0, 0.0).astype(bf16)
        return carry

    lax.fori_loop(0, chips // 2, build_nodes, 0)
    update(receive(2))

    loads[5].wait()
    weight = oweight_ref[o]
    obj_copies = []
    for s in [n_obj // 2, *(s for s in range(1, n_obj) if s != n_obj // 2), 0]:
        q = lax.rem(o + s, n_obj)

        first = q * (qrows // 2)
        values = [gathered(surf_hot[first + k], surf_mask[first + k]) for k in range(qrows // 2)]
        for k, value in enumerate(values):
            lanes = pl.ds(pl.multiple_of((first + k) * WIDE, WIDE), WIDE)
            part = grad[0, :, lanes] * value[0:1]
            for f in range(1, fields):
                part = part + grad[f, :, lanes] * value[f : f + 1]
            part = part * weight
            ssend[s, 2 * k] = part[:, 0:LANES]
            ssend[s, 2 * k + 1] = part[:, LANES:WIDE]
        if s:
            copy = pltpu.make_async_remote_copy(
                src_ref=ssend.at[s],
                dst_ref=srecv.at[s - 1],
                send_sem=obj_send.at[s - 1],
                recv_sem=obj_recv.at[s - 1],
                device_id={"obj": q},
            )
            copy.start()
            obj_copies.append(copy)
    for copy in obj_copies:
        copy.wait_recv()
    comb[...] = ssend[0] + srecv[0] + srecv[1] + srecv[2]
    combined = jnp.concatenate([comb[:, c, :] for c in range(comps)], axis=0)
    high, low = halves(combined)
    vhl[:, 0:LANES] = high.astype(bf16)
    vhl[:, LANES:WIDE] = low.astype(bf16)

    def pick(first):
        values = []
        for u in range(first, first + BATCH):
            found = dot(vhl[...], relay_hot[u]).reshape(comps, qrows, WIDE)
            values.append(jnp.sum(found * relay_mask[u][None], axis=1))
        for u, value in enumerate(values, first):
            vsend[2 * u] = value[:, 0:LANES]
            vsend[2 * u + 1] = value[:, LANES:WIDE]

    relay_send(vsend, vrecv, SWEEPS + 1, pick)

    def place_nodes(u):
        lanes = slice(u * WIDE, (u + 1) * WIDE)
        value = jnp.concatenate(
            [jnp.where(mine, vrecv[4 * u + 2 * k], vrecv[4 * u + 2 * k + 1]) for k in range(2)], axis=1
        )
        mask = fiota((half_nodes, WIDE), 0) == inode[u][0:1]
        for part, these in enumerate(halves(value)):
            for c in range(comps):
                at = (part * comps + c) * half_nodes
                node_lhs[at : at + half_nodes, lanes] = jnp.where(mask, these[c : c + 1], 0.0).astype(bf16)

    forces = None
    for h in (1, 0):
        wait_for(vrecv.at[pl.ds(h * chips, chips)], recv_sem.at[SWEEPS + 1, h])
        for u in range(h * chips // 4, (h + 1) * chips // 4, CHAIN):
            for j in range(CHAIN):
                place_nodes(u + j)
            lanes = slice(u * WIDE, (u + CHAIN) * WIDE)
            part = dot_nt(node_lhs[:, lanes], node_hot[:, lanes])
            forces = part if forces is None else forces + part
    forces = forces[0 : comps * half_nodes] + forces[comps * half_nodes :]
    forces = forces.reshape(comps, size_x // 2, size_y, WIDE)
    force = jnp.concatenate([forces[..., 0:LANES], forces[..., LANES:WIDE]], axis=1)

    scaled = coef[...][None] * force
    first = base[...] + scaled
    mesh1[...] = first
    ysend[1, 0] = mesh1[:, :, size_y - 1, :]
    ysend[1, 1] = mesh1[:, :, 0, :]
    halos1 = halo_copies(1, mesh1)
    for copy in halos1:
        copy.start()
    for copy in halos1:
        copy.wait_recv()
    centre, beside = neighbours(1, mesh1)
    mesh2[...] = (1.0 - OMEGA) * centre + scaled + coef[...][None] * beside

    for copy in halos0 + halos1 + obj_copies:
        copy.wait_send()
    wait_for(sbuf0.at[pl.ds(0, n_blocks - 1)], send_sem.at[0])
    for sweep in range(1, SWEEPS):
        wait_for(sbuf1.at[sweep - 1, pl.ds(0, n_blocks - 1)], send_sem.at[sweep])
    for sb, which in ((irecv, SWEEPS), (vrecv, SWEEPS + 1)):
        wait_for(sb.at[pl.ds(0, n_blocks - 1)], send_sem.at[which])


def write_out(flow, mesh, flow_out, mesh_out, sems):
    copies = [pltpu.make_async_copy(flow, flow_out, sems.at[0]), pltpu.make_async_copy(mesh, mesh_out, sems.at[1])]
    for copy in copies:
        copy.start()
    for copy in copies:
        copy.wait()


def shards(
    n_blocks, n_obj, start, source, binv, coup, send, peer, recv, wgt, scell, grad, oweight, owner, node, mesh, stiff
):
    _, fields, rows_y, cols = start.shape
    faces, surf = send.shape[0], scell.shape[0]
    comps, size_x, size_y, _ = mesh.shape
    quarter = surf // n_obj
    qrows = quarter // LANES
    chips = n_blocks // 2
    half_nodes = size_x * size_y // 2
    vmem = pl.BlockSpec(memory_space=pltpu.VMEM)
    smem = pl.BlockSpec(memory_space=pltpu.SMEM)
    hbm = pl.BlockSpec(memory_space=pl.ANY)
    V = pltpu.VMEM
    dma = pltpu.SemaphoreType.DMA
    call = pl.pallas_call(
        functools.partial(kernel, n_blocks, n_obj, fields, rows_y, faces, surf, comps, size_x, size_y),
        out_shape=(
            V((fields * rows_y, cols), f32),
            V(mesh.shape, f32),
        ),
        in_specs=[hbm] * 10 + [smem] + [hbm] * 4,
        out_specs=(vmem, vmem),
        scratch_shapes=[
            V((fields, rows_y, cols), f32),
            V(binv.shape, f32),
            V(coup.shape, f32),
            V((fields, comps, surf), f32),
            V(mesh.shape, f32),
            V(stiff.shape, f32),
            V((faces // LANES, LANES), i32),
            V((faces // LANES, LANES), i32),
            V((faces // LANES, LANES), i32),
            V((faces // LANES, LANES), f32),
            V((fields, rows_y, cols), f32),
            V((surf // LANES, LANES), i32),
            V((qrows, LANES), i32),
            V((qrows, LANES), i32),
            V((faces // WIDE * n_blocks, 2 * WIDE), bf16),
            V((6 * chips, faces), bf16),
            V((WIDE, faces), bf16),
            V((chips, WIDE), f32),
            V((chips, WIDE), f32),
            V((chips, WIDE), f32),
            V((chips, WIDE, WIDE), bf16),
            V((chips, rows_y, WIDE), f32),
            V((surf // WIDE, WIDE, WIDE), bf16),
            V((surf // WIDE, rows_y, WIDE), f32),
            V((fields * rows_y, WIDE), bf16),
            V((fields, rows_y, LANES), f32),
            V((n_blocks, fields + 1, LANES), f32),
            V((n_blocks, fields + 1, LANES), f32),
            V((SWEEPS - 1, n_blocks, fields, LANES), f32),
            V((SWEEPS - 1, n_blocks, fields, LANES), f32),
            V((WIDE, chips * WIDE), bf16),
            V((fields * rows_y, chips * WIDE), bf16),
            V((n_obj, qrows, comps, LANES), f32),
            V((n_obj - 1, qrows, comps, LANES), f32),
            V((qrows, comps, LANES), f32),
            V((comps * qrows, WIDE), bf16),
            V((chips, 1, WIDE), i32),
            V((chips, LANES), f32),
            V((chips, LANES), f32),
            V((chips // 2, WIDE, WIDE), bf16),
            V((chips // 2, qrows, WIDE), f32),
            V((chips, 2, LANES), f32),
            V((n_blocks, 2, LANES), f32),
            V((chips, comps, LANES), f32),
            V((n_blocks, comps, LANES), f32),
            V((WIDE, chips * LANES), bf16),
            V((2 * comps * half_nodes, chips * LANES), bf16),
            V((chips // 2, 2, WIDE), f32),
            V(mesh.shape, f32),
            V(mesh.shape, f32),
            V(stiff.shape, f32),
            V((2, 2, comps, size_x, LANES), f32),
            V((2, 2, comps, size_x, LANES), f32),
            V((2, 2, comps, size_y, LANES), f32),
            dma((14,)),
            dma((SWEEPS + 2,)),
            dma((SWEEPS + 2, GROUPS)),
            dma((n_obj - 1,)),
            dma((n_obj - 1,)),
            dma((2, 4)),
            dma((2, 4)),
        ],
        compiler_params=pltpu.CompilerParams(
            collective_id=0, has_side_effects=True, vmem_limit_bytes=56 * 1024 * 1024
        ),
    )
    flow, mesh_adjoint = call(
        start[0],
        source[0],
        binv,
        coup,
        send.reshape(-1, LANES),
        peer.reshape(-1, LANES),
        recv.reshape(-1, LANES),
        wgt.reshape(-1, LANES),
        scell.reshape(-1, LANES),
        jnp.transpose(grad, (1, 0, 2)),
        oweight,
        owner.reshape(-1, LANES),
        node.reshape(-1, LANES),
        mesh,
        stiff,
    )
    flow, mesh_adjoint = pl.pallas_call(
        write_out,
        out_shape=(jax.ShapeDtypeStruct(flow.shape, f32), jax.ShapeDtypeStruct(mesh.shape, f32)),
        in_specs=[vmem, vmem],
        out_specs=(hbm, hbm),
        scratch_shapes=[dma((2,))],
    )(
        pltpu.with_memory_space_constraint(flow, pltpu.VMEM),
        pltpu.with_memory_space_constraint(mesh_adjoint, pltpu.VMEM),
    )
    return flow.reshape(start.shape), mesh_adjoint


def solution(mesh):
    placed = (
        P("obj", None, "blocks", None),
        P("obj", None, "blocks", None),
        P(None, None, "blocks", None),
        P(None, "blocks", None),
        P("blocks"),
        P("blocks", None),
        P("blocks"),
        P("blocks"),
        P("blocks"),
        P(None, None, "blocks"),
        P(),
        P(("blocks", "obj"), None),
        P(("blocks", "obj")),
        P(None, "blocks", "obj", None),
        P("blocks", "obj", None),
    )
    return jax.shard_map(
        functools.partial(shards, mesh.shape["blocks"], mesh.shape["obj"]),
        mesh=mesh,
        in_specs=placed,
        out_specs=(P("obj", None, "blocks", None), P(None, "blocks", "obj", None)),
        check_vma=False,
    )
```
